32 devices in a mesh: row: 4 (over y, core), col: 4 (over z), aux: 2 (over x).
Axes of the slice: x: 2, y: 2, z: 4, core: 2. Of those that a mesh axis runs over, the one named last changes fastest.
Arguments:
- integrals: bfloat16 [2, 128, 64, 3072], P('aux', ('row', 'col')), may hold values from -0.75 to 0.75
- block_mask: int32 [2, 64, 64], P('aux', ('row', 'col')), may hold values from 0 to 1, as said below
- block_slots: int32 [2, 64, 64], P('aux', ('row', 'col')), may hold values from -1 to 7, as said below
- orbitals: bfloat16 [64, 4096], replicated, may hold values from -0.21582031 to 0.21582031
Outputs:
- exchange_matrix: float32 [4096, 4, 1024], P(('row', 'aux'), None, 'col')
The draws below stay inside these ranges and needn't reach their ends.
Inputs may be any that keep to these rules, and one draw needn't show every extreme that they name: `block_mask`: within one device's tile (one auxiliary batch, the mu blocks of one row and col index pair, all lambda blocks) between 1 and 8 blocks survive, and in some tile exactly 8. `block_slots`: the surviving blocks of a tile are numbered 0, 1, 2, ... in row-major order of (mu block, lambda block); blocks that did not survive hold -1, and packed slots past a tile's count hold data that is never read.
All inputs are finite; a program needn't handle non-finite values.
Results may differ from the reference program's by a relative error of at most 0.0017.
Values may be sent and summed in bfloat16 or wider, within the bound.
A program may use at most 128 MiB of HBM per device.

```python
import jax
import jax.numpy as jnp
from jax import lax

NBAS = 4096
BLK = 64
NOCC = 64
QDEV = 48
CAP = 8
NMB = 64
MB_DEV = 4
N_ROW = 4
N_COL = 4
N_AUX = 2


def screened_layout(key):
    tiles = N_AUX * N_ROW * N_COL
    positions = NMB // (N_ROW * N_COL) * NMB
    count_key, pick_key, order_key = jax.random.split(key, 3)
    counts = jax.random.randint(count_key, (tiles,), 1, CAP + 1)
    busiest = jax.random.randint(pick_key, (), 0, tiles)
    counts = jnp.where(jnp.arange(tiles) == busiest, CAP, counts)

    def ranking(tile_key):
        return jax.random.permutation(tile_key, positions)
    ranks = jax.vmap(ranking)(jax.random.split(order_key, tiles))
    present = (ranks < counts[:, None]).astype(jnp.int32)
    before = jnp.cumsum(present, axis=1) - present
    slots = jnp.where(present == 1, before, -1).astype(jnp.int32)
    return (present.reshape(N_AUX, NMB, NMB), slots.reshape(N_AUX, NMB, NMB))


def draw_block_mask(key, part):
    present, slots = screened_layout(key)
    return present


def draw_block_slots(key, part):
    present, slots = screened_layout(key)
    return slots


def steps_of(rng, shape, shards, low, top_value):
    factor_of, own = 1.0, jax.random.fold_in(rng, 6)
    for axis_at, shards_of in shards:
        heights = jnp.exp(jax.random.uniform(jax.random.fold_in(own, axis_at), (shards_of,), jnp.float32, low / len(shards), top_value / len(shards)))
        factor_of = factor_of * jnp.repeat(heights, shape[axis_at] // shards_of).reshape([-1 if axis == axis_at else 1 for axis in range(len(shape))])
    return factor_of


def centred(own_key, shape, width, limit, shards=(), kind=jnp.bfloat16):
    values = jax.random.normal(own_key, shape, jnp.float32) * width
    if len(shards) > 0:
        values = steps_of(own_key, shape, shards, -0.22, 0.18) * values
    return jnp.clip(values, min=-limit, max=limit).astype(kind)


def setup_inputs(seed: int = 0) -> dict:
    key_list = jax.random.split(jax.random.key(seed), 5)
    integrals = centred(key_list[0], (N_AUX, N_ROW * N_COL * CAP, BLK, QDEV * BLK), 0.125, 0.75, ((0, 2), (1, 16)))
    block_mask = draw_block_mask(jax.random.fold_in(key_list[4], 71), 0)
    block_slots = draw_block_slots(jax.random.fold_in(key_list[4], 71), 0)
    orbitals = centred(key_list[3], (NOCC, NBAS), ((8.0 / (QDEV * N_AUX * NOCC)) ** 0.5), 0.21582031)
    return {"integrals": integrals, "block_mask": block_mask, "block_slots": block_slots, "orbitals": orbitals}


def half_transform(mask_tile, slot_tile, packed_tile, orbitals):
    capacity = packed_tile.shape[0]
    block_size = packed_tile.shape[1]
    row_blocks, block_count = mask_tile.shape
    occ_count = orbitals.shape[0]
    aux_count = packed_tile.shape[2] // block_size
    mask_flat = mask_tile.reshape(-1)
    slot_flat = slot_tile.reshape(-1)
    positions = jnp.arange(mask_flat.shape[0], dtype=jnp.int32)
    slot_ids = jnp.arange(capacity, dtype=jnp.int32)
    select = ((mask_flat[None, :] == 1) & (slot_flat[None, :] == slot_ids[:, None])).astype(jnp.int32)
    block_row = jnp.sum(select * (positions // block_count)[None, :], axis=1).astype(jnp.int32)
    lam_block = jnp.sum(select * (positions % block_count)[None, :], axis=1).astype(jnp.int32)
    present = jnp.sum(select, axis=1).astype(jnp.float32)
    weights = (block_row[:, None] == jnp.arange(row_blocks, dtype=jnp.int32)[None, :]).astype(jnp.float32) * present[:, None]
    orbital_blocks = jnp.take(orbitals.reshape(occ_count, block_count, block_size), lam_block, axis=1)
    products = jnp.einsum("isx,sxy->siy", orbital_blocks.astype(jnp.float32), packed_tile.astype(jnp.float32), precision=lax.Precision.HIGHEST)
    products = products.reshape(capacity, occ_count, aux_count, block_size)
    half_block = jnp.einsum("sb,siqm->iqbm", weights, products, precision=lax.Precision.HIGHEST)
    return half_block.reshape(occ_count, aux_count, row_blocks * block_size).astype(jnp.bfloat16)


def reference(integrals, block_mask, block_slots, orbitals):
    tiles = N_ROW * N_COL
    masks = block_mask.reshape(N_AUX, tiles, MB_DEV, NMB)
    slots = block_slots.reshape(N_AUX, tiles, MB_DEV, NMB)
    packed = integrals.reshape(N_AUX, tiles, CAP, BLK, QDEV * BLK)

    def per_batch(running_sum, batch_items):
        mask_batch, slot_batch, packed_batch = batch_items
        blocks = jax.vmap(half_transform, in_axes=(0, 0, 0, None))(mask_batch, slot_batch, packed_batch, orbitals)
        whole = jnp.transpose(blocks, (1, 2, 0, 3)).reshape(NOCC * QDEV, NBAS).astype(jnp.float32)
        return running_sum + jnp.dot(whole.T, whole, precision=lax.Precision.HIGHEST), None

    total, unused = lax.scan(per_batch, jnp.zeros((NBAS, NBAS), jnp.float32), (masks, slots, packed))
    return total.reshape(NBAS, N_ROW, NBAS // N_ROW)
```

```python
import functools

import jax
import jax.numpy as jnp
from jax import lax
from jax.experimental import pallas as pl
from jax.experimental.pallas import tpu as pltpu
from jax.sharding import PartitionSpec as P

MESH = pl.DeviceIdType.MESH
LANES = 128


def weigh(dims, mask_ref, slot_ref, orb_ref, weights):
    MB, OCC, BLK, CAP = dims
    mask, slot = mask_ref[...], slot_ref[...]
    lane_count = mask.shape[1]
    row_ids = lax.broadcasted_iota(jnp.int32, mask.shape, 0)
    lam_ids = lax.broadcasted_iota(jnp.int32, mask.shape, 1)
    code = row_ids * lane_count + lam_ids
    low = lax.broadcasted_iota(jnp.int32, (OCC, LANES), 1) < BLK

    def slot_block(s, half):
        select = jnp.where((mask == 1) & (slot == s), 1, 0)
        position = jnp.sum(select * (code + 1))
        present = jnp.minimum(position, 1)
        place = jnp.maximum(position - 1, 0)
        lam, row = place % lane_count, place // lane_count
        start = pl.multiple_of((lam // 2) * LANES, LANES)
        values = orb_ref[:, pl.ds(start, LANES)].astype(jnp.float32)
        odd = lam % 2
        values = jnp.where(odd == half, values, pltpu.roll(values, BLK, 1))
        return values, row, present

    for p in range(CAP // 2):
        lo, lo_row, lo_here = slot_block(2 * p, 0)
        hi, hi_row, hi_here = slot_block(2 * p + 1, 1)
        for b in range(MB):
            lo_w = jnp.where(lo_row == b, lo_here, 0).astype(jnp.float32)
            hi_w = jnp.where(hi_row == b, hi_here, 0).astype(jnp.float32)
            weights[b * OCC : (b + 1) * OCC, p * LANES : (p + 1) * LANES] = jnp.where(
                low, lo * lo_w, hi * hi_w
            ).astype(jnp.bfloat16)


def kernel(
    dims,
    packed_ref,
    weights,
    out_ref,
    panel,
    column,
    block,
    kept,
    send_sum,
    send_turn,
    recv_sum,
    recv_turn,
    z_recv,
    z_up,
    z_down,
    row_recv,
    row_send,
    sum_send,
    sum_recv,
    turn_send,
    turn_recv,
):
    R, C, A, MB, OCC, BLK, CAP, KDIM, PIECES = dims
    T = MB * BLK
    NH = T // LANES
    NT = C // A
    half_c = C // 2
    step = KDIM // PIECES
    r, c, a = lax.axis_index("row"), lax.axis_index("col"), lax.axis_index("aux")
    devices = R * C * A
    me = (r * C + c) * A + a

    barrier = pltpu.get_barrier_semaphore()

    def greet(k, _):
        @pl.when(k != me)
        def _():
            pl.semaphore_signal(
                barrier,
                inc=1,
                device_id={"row": k // (C * A), "col": (k // A) % C, "aux": k % A},
                device_id_type=MESH,
            )

        return 0

    lax.fori_loop(0, devices, greet, 0)

    low = lax.broadcasted_iota(jnp.int32, (OCC, LANES), 1) < BLK

    def transform(g, _):
        at = pl.multiple_of(g * 256, 256)
        h = jnp.dot(
            weights[...], packed_ref[:, pl.ds(at, 256)], preferred_element_type=jnp.float32
        )
        for j in range(2):
            for hh in range(NH):
                b0 = h[2 * hh * OCC : (2 * hh + 1) * OCC, j * LANES : (j + 1) * LANES]
                b1 = h[(2 * hh + 1) * OCC : (2 * hh + 2) * OCC, j * LANES : (j + 1) * LANES]
                even = jnp.where(low, b0, pltpu.roll(b1, BLK, 1)).astype(jnp.bfloat16)
                odd = jnp.where(low, pltpu.roll(b0, BLK, 1), b1).astype(jnp.bfloat16)
                first = pl.multiple_of((g * 4 + 2 * j) * OCC, OCC)
                second = pl.multiple_of((g * 4 + 2 * j + 1) * OCC, OCC)
                lanes = slice(hh * LANES, (hh + 1) * LANES)
                panel[c, hh, pl.ds(first, OCC), :] = even
                panel[c, hh, pl.ds(second, OCC), :] = odd
                column[r, pl.ds(first, OCC), lanes] = even
                column[r, pl.ds(second, OCC), lanes] = odd
        return 0

    lax.fori_loop(0, KDIM // 256, transform, 0)

    pl.semaphore_wait(barrier, devices - 1)

    def z_copy(src, hh, p, up):
        ref = panel.at[src, hh, pl.ds(pl.multiple_of(p * step, step), step), :]
        target = jnp.minimum(c + 1, C - 1) if up else jnp.maximum(c - 1, 0)
        index = (src * NH + hh) * PIECES + p
        return pltpu.make_async_remote_copy(
            src_ref=ref,
            dst_ref=ref,
            send_sem=(z_up if up else z_down).at[index],
            recv_sem=z_recv.at[index],
            device_id={"row": r, "col": target, "aux": a},
            device_id_type=MESH,
        )

    def row_copy(tile, target, send_index):
        return pltpu.make_async_remote_copy(
            src_ref=column.at[tile],
            dst_ref=column.at[tile],
            send_sem=row_send.at[send_index],
            recv_sem=row_recv.at[tile],
            device_id={"row": target, "col": c, "aux": a},
            device_id_type=MESH,
        )

    def each_piece(act):
        lax.fori_loop(0, PIECES, lambda p, _: (act(p), 0)[1], 0)

    sends_up = (c < half_c) & (c + 1 < C)
    sends_down = c - 1 >= half_c
    sibling = r + 1 - 2 * (r % 2)
    pairs = R // 2
    peers = [(r + 2 * j) % R for j in range(pairs)]
    far = [(sibling + 2 * j) % R for j in range(pairs)]

    for j in range(1, pairs):
        row_copy(r, peers[j], j).start()
    row_copy(r, sibling, 0).start()
    for hh in range(NH):

        @pl.when(sends_up)
        def _():
            each_piece(lambda p: z_copy(c, hh, p, True).start())

        @pl.when(sends_down)
        def _():
            each_piece(lambda p: z_copy(c, hh, p, False).start())

    def has_up(src):
        return (src >= 0) & (src < half_c)

    def has_down(src):
        return (src < C) & (c >= half_c)

    def take(src, hh, p, up):
        z_copy(src, hh, p, up).wait_recv()

        @pl.when((c + 1 < C) if up else (c - 1 >= half_c))
        def _():
            z_copy(src, hh, p, up).start()

    for hh in range(NH):

        @pl.when(has_up(c - 1))
        def _():
            each_piece(lambda p: take(c - 1, hh, p, True))

    for j in range(1, pairs):
        row_copy(peers[j], sibling, j).wait_recv()
        row_copy(peers[j], sibling, pairs + j).start()
    for j in range(pairs):
        row_copy(far[j], sibling, 0).wait_recv()

    def sum_copy(src, hh):
        return pltpu.make_async_remote_copy(
            src_ref=send_sum.at[src, hh],
            dst_ref=recv_sum.at[src % NT, a, hh],
            send_sem=sum_send.at[src * NH + hh],
            recv_sem=sum_recv.at[((src % NT) * A + a) * NH + hh],
            device_id={"row": r, "col": c, "aux": src // NT},
            device_id_type=MESH,
        )

    def turn_copy(src, hh, r2):
        return pltpu.make_async_remote_copy(
            src_ref=send_turn.at[src, hh, r2],
            dst_ref=recv_turn.at[c % NT, a, r, hh],
            send_sem=turn_send.at[(src * NH + hh) * R + r2],
            recv_sem=turn_recv.at[(((c % NT) * A + a) * R + r) * NH + hh],
            device_id={"row": r2, "col": src, "aux": c // NT},
            device_id_type=MESH,
        )

    def multiply(src, hh, p, r2):
        rows = pl.ds(pl.multiple_of(p * step, step), step)
        return lax.dot_general(
            panel[src, hh, rows, :],
            column[r2, rows, :],
            (((0,), (0,)), ((), ())),
            preferred_element_type=jnp.float32,
        )

    def product(src, hh, before, turned):
        def piece(p, _):
            before(p)

            def one(r2, _):
                value = multiply(src, hh, p, r2)
                block[r2] = jnp.where(p == 0, value, block[r2] + value)
                return 0

            return lax.fori_loop(0, R, one, 0)

        lax.fori_loop(0, PIECES, piece, 0)

        if turned:

            def turn(r2, _):
                send_turn[src, hh, r2] = block[r2].T.astype(jnp.bfloat16)
                turn_copy(src, hh, r2).start()
                return 0

            lax.fori_loop(0, R, turn, 0)

        @pl.when(src // NT == a)
        def _():
            kept[src % NT, hh] = block[...]

        @pl.when(src // NT != a)
        def _():
            send_sum[src, hh] = block[...].astype(jnp.bfloat16)
            sum_copy(src, hh).start()

    block[...] = jnp.zeros_like(block)
    for hh in range(NH):
        product(c, hh, lambda p: None, False)
    for d in range(1, C):
        for hh in range(NH):

            @pl.when(has_up(c - d))
            def _():
                before = (lambda p: None) if d == 1 else lambda p: take(c - d, hh, p, True)
                product(c - d, hh, before, True)

            @pl.when(has_down(c + d))
            def _():
                product(c + d, hh, lambda p: take(c + d, hh, p, False), True)

    for t in range(NT):
        tile = a * NT + t
        here = (tile == c) | ((tile < c) & (tile < half_c)) | ((tile > c) & (c >= half_c))

        @pl.when(here)
        def _():
            for hh in range(NH):

                def add(other, _):
                    source = (a + other) % A
                    index = (t * A + source) * NH + hh
                    pltpu.make_async_remote_copy(
                        src_ref=recv_sum.at[t, source, hh],
                        dst_ref=recv_sum.at[t, source, hh],
                        send_sem=sum_send.at[0],
                        recv_sem=sum_recv.at[index],
                        device_id={"row": r, "col": c, "aux": source},
                        device_id_type=MESH,
                    ).wait_recv()
                    kept[t, hh] = kept[t, hh] + recv_sum[t, source, hh].astype(jnp.float32)
                    return 0

                lax.fori_loop(1, A, add, 0)
                for r2 in range(R):
                    out_ref[
                        t * T + hh * LANES : t * T + (hh + 1) * LANES, r2 * T : (r2 + 1) * T
                    ] = kept[t, hh, r2]

        @pl.when(jnp.logical_not(here))
        def _():
            for hh in range(NH):
                for r2 in range(R):

                    def add(source, total):
                        index = ((t * A + source) * R + r2) * NH + hh
                        pltpu.make_async_remote_copy(
                            src_ref=recv_turn.at[t, source, r2, hh],
                            dst_ref=recv_turn.at[t, source, r2, hh],
                            send_sem=turn_send.at[0],
                            recv_sem=turn_recv.at[index],
                            device_id={"row": r2, "col": tile, "aux": source},
                            device_id_type=MESH,
                        ).wait_recv()
                        return total + recv_turn[t, source, r2, hh].astype(jnp.float32)

                    out_ref[
                        t * T : (t + 1) * T, r2 * T + hh * LANES : r2 * T + (hh + 1) * LANES
                    ] = lax.fori_loop(0, A, add, jnp.zeros((T, LANES), jnp.float32))

    for j in range(1, pairs):
        row_copy(r, peers[j], j).wait_send()
        row_copy(peers[j], sibling, pairs + j).wait_send()
    row_copy(r, sibling, 0).wait_send()
    for hh in range(NH):

        @pl.when(sends_up)
        def _():
            each_piece(lambda p: z_copy(c, hh, p, True).wait_send())

        @pl.when(sends_down)
        def _():
            each_piece(lambda p: z_copy(c, hh, p, False).wait_send())

    def finish(src, hh, up, turned):
        if turned:

            @pl.when((c + 1 < C) if up else (c - 1 >= half_c))
            def _():
                each_piece(lambda p: z_copy(src, hh, p, up).wait_send())

            lax.fori_loop(0, R, lambda r2, _: (turn_copy(src, hh, r2).wait_send(), 0)[1], 0)

        @pl.when(src // NT != a)
        def _():
            sum_copy(src, hh).wait_send()

    for hh in range(NH):
        finish(c, hh, True, False)
    for d in range(1, C):
        for hh in range(NH):

            @pl.when(has_up(c - d))
            def _():
                finish(c - d, hh, True, True)

            @pl.when(has_down(c + d))
            def _():
                finish(c + d, hh, False, True)


def local(sizes, integrals, block_mask, block_slots, orbitals):
    R, C, A = sizes
    _, cap, blk, width = integrals.shape
    mb = block_mask.shape[1]
    occ = orbitals.shape[0]
    T = mb * blk
    kdim = occ * (width // blk)
    NH, NT, pieces = T // LANES, C // A, 4
    dims = (R, C, A, mb, occ, blk, cap, kdim, pieces)
    dma = pltpu.SemaphoreType.DMA
    bf16, f32 = jnp.bfloat16, jnp.float32
    vmem = pl.BlockSpec(memory_space=pltpu.VMEM)
    weights = pl.pallas_call(
        functools.partial(weigh, (mb, occ, blk, cap)),
        out_shape=jax.ShapeDtypeStruct((mb * occ, cap * blk), bf16),
        in_specs=[vmem] * 3,
        out_specs=vmem,
    )(
        block_mask.reshape(block_mask.shape[1:]),
        block_slots.reshape(block_slots.shape[1:]),
        orbitals,
    )
    result = pl.pallas_call(
        functools.partial(kernel, dims),
        out_shape=jax.ShapeDtypeStruct((NT * T, R * T), f32),
        in_specs=[vmem] * 2,
        out_specs=vmem,
        scratch_shapes=[
            pltpu.VMEM((C, NH, kdim, LANES), bf16),
            pltpu.VMEM((R, kdim, T), bf16),
            pltpu.VMEM((R, LANES, T), f32),
            pltpu.VMEM((NT, NH, R, LANES, T), f32),
            pltpu.VMEM((C, NH, R, LANES, T), bf16),
            pltpu.VMEM((C, NH, R, T, LANES), bf16),
            pltpu.VMEM((NT, A, NH, R, LANES, T), bf16),
            pltpu.VMEM((NT, A, R, NH, T, LANES), bf16),
            dma((C * NH * pieces,)),
            dma((C * NH * pieces,)),
            dma((C * NH * pieces,)),
            dma((R,)),
            dma((R,)),
            dma((C * NH,)),
            dma((NT * A * NH,)),
            dma((C * NH * R,)),
            dma((NT * A * R * NH,)),
        ],
        compiler_params=pltpu.CompilerParams(
            collective_id=0, has_side_effects=True, vmem_limit_bytes=50 * 1024 * 1024
        ),
        cost_estimate=pl.CostEstimate(
            flops=2 * C * T * R * T * kdim, bytes_accessed=8 * 1024 * 1024, transcendentals=0
        ),
    )(
        integrals.reshape(cap * blk, width), weights
    )
    return result.reshape(NT * T, R, T)


def solution(mesh):
    sizes = tuple(mesh.shape[name] for name in ("row", "col", "aux"))
    placed = (
        P("aux", ("row", "col"), None, None),
        P("aux", ("row", "col"), None),
        P("aux", ("row", "col"), None),
        P(),
    )
    return jax.shard_map(
        functools.partial(local, sizes),
        mesh=mesh,
        in_specs=placed,
        out_specs=P(("row", "aux"), None, "col"),
        check_vma=False,
    )
```

```python
import functools

import jax
import jax.numpy as jnp
from jax import lax
from jax.experimental import pallas as pl
from jax.experimental.pallas import tpu as pltpu
from jax.sharding import PartitionSpec as P

MESH = pl.DeviceIdType.MESH
LANES = 128


def weigh(dims, mask_ref, slot_ref, orb_ref, weights):
    MB, OCC, BLK, CAP = dims
    mask, slot = mask_ref[...], slot_ref[...]
    lane_count = mask.shape[1]
    row_ids = lax.broadcasted_iota(jnp.int32, mask.shape, 0)
    lam_ids = lax.broadcasted_iota(jnp.int32, mask.shape, 1)
    code = row_ids * lane_count + lam_ids
    low = lax.broadcasted_iota(jnp.int32, (OCC, LANES), 1) < BLK

    def slot_block(s, half):
        select = jnp.where((mask == 1) & (slot == s), 1, 0)
        position = jnp.sum(select * (code + 1))
        present = jnp.minimum(position, 1)
        place = jnp.maximum(position - 1, 0)
        lam, row = place % lane_count, place // lane_count
        start = pl.multiple_of((lam // 2) * LANES, LANES)
        values = orb_ref[:, pl.ds(start, LANES)].astype(jnp.float32)
        odd = lam % 2
        values = jnp.where(odd == half, values, pltpu.roll(values, BLK, 1))
        return values, row, present

    for p in range(CAP // 2):
        lo, lo_row, lo_here = slot_block(2 * p, 0)
        hi, hi_row, hi_here = slot_block(2 * p + 1, 1)
        for b in range(MB):
            lo_w = jnp.where(lo_row == b, lo_here, 0).astype(jnp.float32)
            hi_w = jnp.where(hi_row == b, hi_here, 0).astype(jnp.float32)
            weights[b * OCC : (b + 1) * OCC, p * LANES : (p + 1) * LANES] = jnp.where(
                low, lo * lo_w, hi * hi_w
            ).astype(jnp.bfloat16)


def kernel(
    dims,
    packed_ref,
    weights,
    out_ref,
    panel,
    column,
    block,
    kept,
    send,
    recv_sum,
    recv_turn,
    z_recv,
    z_up,
    z_down,
    row_recv,
    row_send,
    sum_send,
    sum_recv,
    turn_send,
    turn_recv,
):
    R, C, A, MB, OCC, BLK, CAP, KDIM, PIECES = dims
    T = MB * BLK
    NH = T // LANES
    NT = C // A
    half_c = C // 2
    step = KDIM // PIECES
    r, c, a = lax.axis_index("row"), lax.axis_index("col"), lax.axis_index("aux")
    devices = R * C * A
    me = (r * C + c) * A + a

    barrier = pltpu.get_barrier_semaphore()

    def greet(k, _):
        @pl.when(k != me)
        def _():
            pl.semaphore_signal(
                barrier,
                inc=1,
                device_id={"row": k // (C * A), "col": (k // A) % C, "aux": k % A},
                device_id_type=MESH,
            )

        return 0

    lax.fori_loop(0, devices, greet, 0)

    low = lax.broadcasted_iota(jnp.int32, (OCC, LANES), 1) < BLK

    def transform(g, _):
        at = pl.multiple_of(g * 256, 256)
        h = jnp.dot(
            weights[...], packed_ref[:, pl.ds(at, 256)], preferred_element_type=jnp.float32
        )
        for hh in range(NH):
            parts = []
            for j in range(2):
                b0 = h[2 * hh * OCC : (2 * hh + 1) * OCC, j * LANES : (j + 1) * LANES]
                b1 = h[(2 * hh + 1) * OCC : (2 * hh + 2) * OCC, j * LANES : (j + 1) * LANES]
                parts.append(jnp.where(low, b0, pltpu.roll(b1, BLK, 1)))
                parts.append(jnp.where(low, pltpu.roll(b0, BLK, 1), b1))
            tile = jnp.concatenate(parts, axis=0)
            panel[c, hh, pl.ds(at, 256), :] = tile.astype(jnp.bfloat16)
            column[r, hh * LANES : (hh + 1) * LANES, pl.ds(at, 256)] = tile.T.astype(jnp.bfloat16)
        return 0

    lax.fori_loop(0, KDIM // 256, transform, 0)

    pl.semaphore_wait(barrier, devices - 1)

    def z_copy(src, hh, p, up):
        ref = panel.at[src, hh, pl.ds(pl.multiple_of(p * step, step), step), :]
        target = jnp.minimum(c + 1, C - 1) if up else jnp.maximum(c - 1, 0)
        index = (src * NH + hh) * PIECES + p
        return pltpu.make_async_remote_copy(
            src_ref=ref,
            dst_ref=ref,
            send_sem=(z_up if up else z_down).at[index],
            recv_sem=z_recv.at[index],
            device_id={"row": r, "col": target, "aux": a},
            device_id_type=MESH,
        )

    def row_copy(tile, target, send_index):
        return pltpu.make_async_remote_copy(
            src_ref=column.at[tile],
            dst_ref=column.at[tile],
            send_sem=row_send.at[send_index],
            recv_sem=row_recv.at[tile],
            device_id={"row": target, "col": c, "aux": a},
            device_id_type=MESH,
        )

    def each_piece(act):
        lax.fori_loop(0, PIECES, lambda p, _: (act(p), 0)[1], 0)

    sends_up = (c < half_c) & (c + 1 < C)
    sends_down = c - 1 >= half_c
    sibling = r + 1 - 2 * (r % 2)
    pairs = R // 2
    peers = [(r + 2 * j) % R for j in range(pairs)]
    far = [(sibling + 2 * j) % R for j in range(pairs)]

    for j in range(1, pairs):
        row_copy(r, peers[j], j).start()
    row_copy(r, sibling, 0).start()
    for hh in range(NH):

        @pl.when(sends_up)
        def _():
            each_piece(lambda p: z_copy(c, hh, p, True).start())

        @pl.when(sends_down)
        def _():
            each_piece(lambda p: z_copy(c, hh, p, False).start())

    def has_up(src):
        return (src >= 0) & (src < half_c)

    def has_down(src):
        return (src < C) & (c >= half_c)

    def take(src, hh, p, up):
        z_copy(src, hh, p, up).wait_recv()

        @pl.when((c + 1 < C) if up else (c - 1 >= half_c))
        def _():
            z_copy(src, hh, p, up).start()

    passes_down = c - 1 >= half_c
    for hh in range(NH):

        @pl.when(has_up(c - 1))
        def _():
            each_piece(lambda p: take(c - 1, hh, p, True))

        @pl.when(has_down(c + 1) & passes_down)
        def _():
            each_piece(lambda p: take(c + 1, hh, p, False))

    for j in range(1, pairs):
        row_copy(peers[j], sibling, j).wait_recv()
        row_copy(peers[j], sibling, pairs + j).start()
    for j in range(pairs):
        row_copy(far[j], sibling, 0).wait_recv()

    def sum_copy(src, hh):
        return pltpu.make_async_remote_copy(
            src_ref=send.at[src, hh],
            dst_ref=recv_sum.at[src % NT, a, hh],
            send_sem=sum_send.at[src * NH + hh],
            recv_sem=sum_recv.at[((src % NT) * A + a) * NH + hh],
            device_id={"row": r, "col": c, "aux": src // NT},
            device_id_type=MESH,
        )

    def turn_copy(src, hh, r2):
        return pltpu.make_async_remote_copy(
            src_ref=send.at[src, hh, r2],
            dst_ref=recv_turn.at[c % NT, a, r, hh],
            send_sem=turn_send.at[(src * NH + hh) * R + r2],
            recv_sem=turn_recv.at[(((c % NT) * A + a) * R + r) * NH + hh],
            device_id={"row": r2, "col": src, "aux": c // NT},
            device_id_type=MESH,
        )

    def settle(src, hh, r2, value, turned):
        send[src, hh, r2] = value.astype(jnp.bfloat16)
        if turned:
            turn_copy(src, hh, r2).start()

        @pl.when(src // NT == a)
        def _():
            kept[src % NT, hh, r2] = value

    def pass_sum(src, hh):
        @pl.when(src // NT != a)
        def _():
            sum_copy(src, hh).start()

    def whole(src, turned):
        def one(r2, _):
            tile = jnp.concatenate([panel[src, hh] for hh in range(NH)], axis=1)
            value = jnp.dot(column[r2], tile, preferred_element_type=jnp.float32)
            for hh in range(NH):
                settle(src, hh, r2, value[:, hh * LANES : (hh + 1) * LANES], turned)
            return 0

        lax.fori_loop(0, R, one, 0)
        for hh in range(NH):
            pass_sum(src, hh)

    def streamed(src, hh, up):
        def piece(p, _):
            take(src, hh, p, up)
            rows = pl.ds(pl.multiple_of(p * step, step), step)
            for r2 in range(R):
                value = jnp.dot(
                    column[r2, :, rows],
                    panel[src, hh, rows, :],
                    preferred_element_type=jnp.float32,
                )
                block[r2] = jnp.where(p == 0, value, block[r2] + value)
            return 0

        lax.fori_loop(0, PIECES, piece, 0)

        def one(r2, _):
            settle(src, hh, r2, block[r2], True)
            return 0

        lax.fori_loop(0, R, one, 0)
        pass_sum(src, hh)

    block[...] = jnp.zeros_like(block)
    whole(c, False)

    @pl.when(has_up(c - 1))
    def _():
        whole(c - 1, True)

    def nearest_down():
        @pl.when(has_down(c + 1))
        def _():
            @pl.when(jnp.logical_not(passes_down))
            def _():
                for hh in range(NH):
                    each_piece(lambda p: z_copy(c + 1, hh, p, False).wait_recv())

            whole(c + 1, True)

    for d in range(2, C):
        for hh in range(NH):

            @pl.when(has_up(c - d))
            def _():
                streamed(c - d, hh, True)

            if d == 2 and hh == 0:
                nearest_down()

            @pl.when(has_down(c + d))
            def _():
                streamed(c + d, hh, False)

    if C == 2:
        nearest_down()

    for t in range(NT):
        tile = a * NT + t
        here = (tile == c) | ((tile < c) & (tile < half_c)) | ((tile > c) & (c >= half_c))

        @pl.when(here)
        def _():
            for hh in range(NH):

                def arrived(other, _):
                    source = (a + other) % A
                    index = (t * A + source) * NH + hh
                    pltpu.make_async_remote_copy(
                        src_ref=recv_sum.at[t, source, hh],
                        dst_ref=recv_sum.at[t, source, hh],
                        send_sem=sum_send.at[0],
                        recv_sem=sum_recv.at[index],
                        device_id={"row": r, "col": c, "aux": source},
                        device_id_type=MESH,
                    ).wait_recv()
                    kept[t, hh] = kept[t, hh] + recv_sum[t, source, hh].astype(jnp.float32)
                    return 0

                lax.fori_loop(1, A, arrived, 0)
                for r2 in range(R):
                    out_ref[
                        t * T + hh * LANES : t * T + (hh + 1) * LANES, r2 * T : (r2 + 1) * T
                    ] = kept[t, hh, r2].T

        @pl.when(jnp.logical_not(here))
        def _():
            for hh in range(NH):
                for r2 in range(R):

                    def add(source, total):
                        index = ((t * A + source) * R + r2) * NH + hh
                        pltpu.make_async_remote_copy(
                            src_ref=recv_turn.at[t, source, r2, hh],
                            dst_ref=recv_turn.at[t, source, r2, hh],
                            send_sem=turn_send.at[0],
                            recv_sem=turn_recv.at[index],
                            device_id={"row": r2, "col": tile, "aux": source},
                            device_id_type=MESH,
                        ).wait_recv()
                        return total + recv_turn[t, source, r2, hh].astype(jnp.float32)

                    out_ref[
                        t * T : (t + 1) * T, r2 * T + hh * LANES : r2 * T + (hh + 1) * LANES
                    ] = lax.fori_loop(0, A, add, jnp.zeros((T, LANES), jnp.float32))

    for j in range(1, pairs):
        row_copy(r, peers[j], j).wait_send()
        row_copy(peers[j], sibling, pairs + j).wait_send()
    row_copy(r, sibling, 0).wait_send()
    for hh in range(NH):

        @pl.when(sends_up)
        def _():
            each_piece(lambda p: z_copy(c, hh, p, True).wait_send())

        @pl.when(sends_down)
        def _():
            each_piece(lambda p: z_copy(c, hh, p, False).wait_send())

    def finish(src, hh, up, turned):
        if turned:

            @pl.when((c + 1 < C) if up else (c - 1 >= half_c))
            def _():
                each_piece(lambda p: z_copy(src, hh, p, up).wait_send())

            lax.fori_loop(0, R, lambda r2, _: (turn_copy(src, hh, r2).wait_send(), 0)[1], 0)

        @pl.when(src // NT != a)
        def _():
            sum_copy(src, hh).wait_send()

    for hh in range(NH):
        finish(c, hh, True, False)
    for d in range(1, C):
        for hh in range(NH):

            @pl.when(has_up(c - d))
            def _():
                finish(c - d, hh, True, True)

            @pl.when(has_down(c + d))
            def _():
                finish(c + d, hh, False, True)


def local(sizes, integrals, block_mask, block_slots, orbitals):
    R, C, A = sizes
    _, cap, blk, width = integrals.shape
    mb = block_mask.shape[1]
    occ = orbitals.shape[0]
    T = mb * blk
    kdim = occ * (width // blk)
    NH, NT, pieces = T // LANES, C // A, 4
    dims = (R, C, A, mb, occ, blk, cap, kdim, pieces)
    dma = pltpu.SemaphoreType.DMA
    bf16, f32 = jnp.bfloat16, jnp.float32
    vmem = pl.BlockSpec(memory_space=pltpu.VMEM)
    weights = pl.pallas_call(
        functools.partial(weigh, (mb, occ, blk, cap)),
        out_shape=jax.ShapeDtypeStruct((mb * occ, cap * blk), bf16),
        in_specs=[vmem] * 3,
        out_specs=vmem,
    )(
        block_mask.reshape(block_mask.shape[1:]),
        block_slots.reshape(block_slots.shape[1:]),
        orbitals,
    )
    result = pl.pallas_call(
        functools.partial(kernel, dims),
        out_shape=jax.ShapeDtypeStruct((NT * T, R * T), f32),
        in_specs=[vmem] * 2,
        out_specs=vmem,
        scratch_shapes=[
            pltpu.VMEM((C, NH, kdim, LANES), bf16),
            pltpu.VMEM((R, T, kdim), bf16),
            pltpu.VMEM((R, T, LANES), f32),
            pltpu.VMEM((NT, NH, R, T, LANES), f32),
            pltpu.VMEM((C, NH, R, T, LANES), bf16),
            pltpu.VMEM((NT, A, NH, R, T, LANES), bf16),
            pltpu.VMEM((NT, A, R, NH, T, LANES), bf16),
            dma((C * NH * pieces,)),
            dma((C * NH * pieces,)),
            dma((C * NH * pieces,)),
            dma((R,)),
            dma((R,)),
            dma((C * NH,)),
            dma((NT * A * NH,)),
            dma((C * NH * R,)),
            dma((NT * A * R * NH,)),
        ],
        compiler_params=pltpu.CompilerParams(
            collective_id=0, has_side_effects=True, vmem_limit_bytes=50 * 1024 * 1024
        ),
        cost_estimate=pl.CostEstimate(
            flops=2 * C * T * R * T * kdim, bytes_accessed=8 * 1024 * 1024, transcendentals=0
        ),
    )(
        integrals.reshape(cap * blk, width), weights
    )
    return result.reshape(NT * T, R, T)


def solution(mesh):
    sizes = tuple(mesh.shape[name] for name in ("row", "col", "aux"))
    placed = (
        P("aux", ("row", "col"), None, None),
        P("aux", ("row", "col"), None),
        P("aux", ("row", "col"), None),
        P(),
    )
    return jax.shard_map(
        functools.partial(local, sizes),
        mesh=mesh,
        in_specs=placed,
        out_specs=P(("row", "aux"), None, "col"),
        check_vma=False,
    )
```

```python
import functools

import jax
import jax.numpy as jnp
from jax import lax
from jax.experimental import pallas as pl
from jax.experimental.pallas import tpu as pltpu
from jax.sharding import PartitionSpec as P

MESH = pl.DeviceIdType.MESH
LANES = 128


def weigh(dims, mask_ref, slot_ref, orb_ref, weights):
    MB, OCC, BLK, CAP = dims
    mask, slot = mask_ref[...], slot_ref[...]
    lane_count = mask.shape[1]
    row_ids = lax.broadcasted_iota(jnp.int32, mask.shape, 0)
    lam_ids = lax.broadcasted_iota(jnp.int32, mask.shape, 1)
    code = row_ids * lane_count + lam_ids
    low = lax.broadcasted_iota(jnp.int32, (OCC, LANES), 1) < BLK

    def slot_block(s, half):
        select = jnp.where((mask == 1) & (slot == s), 1, 0)
        position = jnp.sum(select * (code + 1))
        present = jnp.minimum(position, 1)
        place = jnp.maximum(position - 1, 0)
        lam, row = place % lane_count, place // lane_count
        start = pl.multiple_of((lam // 2) * LANES, LANES)
        values = orb_ref[:, pl.ds(start, LANES)].astype(jnp.float32)
        odd = lam % 2
        values = jnp.where(odd == half, values, pltpu.roll(values, BLK, 1))
        return values, row, present

    for p in range(CAP // 2):
        lo, lo_row, lo_here = slot_block(2 * p, 0)
        hi, hi_row, hi_here = slot_block(2 * p + 1, 1)
        for b in range(MB):
            lo_w = jnp.where(lo_row == b, lo_here, 0).astype(jnp.float32)
            hi_w = jnp.where(hi_row == b, hi_here, 0).astype(jnp.float32)
            weights[b * OCC : (b + 1) * OCC, p * LANES : (p + 1) * LANES] = jnp.where(
                low, lo * lo_w, hi * hi_w
            ).astype(jnp.bfloat16)


def kernel(
    dims,
    packed_hbm,
    weights,
    out_ref,
    packed_ref,
    panel,
    column,
    kept,
    send,
    recv_sum,
    send_turn,
    recv_turn,
    load,
    z_recv,
    z_up,
    z_down,
    row_recv,
    row_send,
    sum_send,
    sum_recv,
    turn_send,
    turn_recv,
):
    R, C, A, MB, OCC, BLK, CAP, KDIM, PIECES = dims
    T = MB * BLK
    NH = T // LANES
    NT = C // A
    half_c = C // 2
    step = KDIM // PIECES
    r, c, a = lax.axis_index("row"), lax.axis_index("col"), lax.axis_index("aux")
    devices = R * C * A
    me = (r * C + c) * A + a

    loading = pltpu.make_async_copy(packed_hbm, packed_ref, load)
    loading.start()
    barrier = pltpu.get_barrier_semaphore()

    def greet(k, _):
        @pl.when(k != me)
        def _():
            pl.semaphore_signal(
                barrier,
                inc=1,
                device_id={"row": k // (C * A), "col": (k // A) % C, "aux": k % A},
                device_id_type=MESH,
            )

        return 0

    lax.fori_loop(0, devices, greet, 0)

    low = lax.broadcasted_iota(jnp.int32, (OCC, LANES), 1) < BLK

    def transform(g, _):
        at = pl.multiple_of(g * 256, 256)
        h = jnp.dot(
            weights[...], packed_ref[:, pl.ds(at, 256)], preferred_element_type=jnp.float32
        )
        for hh in range(NH):
            parts = []
            for j in range(2):
                b0 = h[2 * hh * OCC : (2 * hh + 1) * OCC, j * LANES : (j + 1) * LANES]
                b1 = h[(2 * hh + 1) * OCC : (2 * hh + 2) * OCC, j * LANES : (j + 1) * LANES]
                parts.append(jnp.where(low, b0, pltpu.roll(b1, BLK, 1)))
                parts.append(jnp.where(low, pltpu.roll(b0, BLK, 1), b1))
            tile = jnp.concatenate(parts, axis=0)
            panel[c, hh, pl.ds(at, 256), :] = tile.astype(jnp.bfloat16)
            column[r, hh * LANES : (hh + 1) * LANES, pl.ds(at, 256)] = tile.T.astype(jnp.bfloat16)
        return 0

    def z_copy(src, hh, p, up):
        ref = panel.at[src, hh, pl.ds(pl.multiple_of(p * step, step), step), :]
        target = jnp.minimum(c + 1, C - 1) if up else jnp.maximum(c - 1, 0)
        index = (src * NH + hh) * PIECES + p
        return pltpu.make_async_remote_copy(
            src_ref=ref,
            dst_ref=ref,
            send_sem=(z_up if up else z_down).at[index],
            recv_sem=z_recv.at[index],
            device_id={"row": r, "col": target, "aux": a},
            device_id_type=MESH,
        )

    def row_copy(tile, target, send_index):
        return pltpu.make_async_remote_copy(
            src_ref=column.at[tile],
            dst_ref=column.at[tile],
            send_sem=row_send.at[send_index],
            recv_sem=row_recv.at[tile],
            device_id={"row": target, "col": c, "aux": a},
            device_id_type=MESH,
        )

    def each_piece(act):
        lax.fori_loop(0, PIECES, lambda p, _: (act(p), 0)[1], 0)

    sends_up = (c < half_c) & (c + 1 < C)
    sends_down = c - 1 >= half_c
    sibling = r + 1 - 2 * (r % 2)
    pairs = R // 2
    peers = [(r + 2 * j) % R for j in range(pairs)]
    far = [(sibling + 2 * j) % R for j in range(pairs)]

    def send_own(hh, p):
        @pl.when(sends_up)
        def _():
            z_copy(c, hh, p, True).start()

        @pl.when(sends_down)
        def _():
            z_copy(c, hh, p, False).start()

    edge = half_c - 1
    loading.wait()
    pl.semaphore_wait(barrier, devices - 1)

    def make_piece(p, _):
        lax.fori_loop(p * (step // 256), (p + 1) * (step // 256), transform, 0)
        send_own(0, p)

        @pl.when(c == edge)
        def _():
            for hh in range(1, NH):
                send_own(hh, p)

        return 0

    lax.fori_loop(0, PIECES, make_piece, 0)
    for j in range(1, pairs):
        row_copy(r, peers[j], j).start()
    row_copy(r, sibling, 0).start()

    @pl.when(c != edge)
    def _():
        for hh in range(1, NH):
            each_piece(lambda p: send_own(hh, p))

    def has_up(src):
        return (src >= 0) & (src < half_c)

    def has_down(src):
        return (src < C) & (c >= half_c)

    def take(src, hh, p, up):
        z_copy(src, hh, p, up).wait_recv()

        @pl.when((c + 1 < C) if up else (c - 1 >= half_c))
        def _():
            z_copy(src, hh, p, up).start()

    passes_down = c - 1 >= half_c

    @pl.when(has_up(c - 1))
    def _():
        def one(n, _):
            by_piece = c - 1 == edge
            hh = jnp.where(by_piece, n % NH, n // PIECES)
            p = jnp.where(by_piece, n // NH, n % PIECES)
            take(c - 1, hh, p, True)
            return 0

        lax.fori_loop(0, NH * PIECES, one, 0)

    @pl.when(has_down(c + 1) & passes_down)
    def _():
        for hh in range(NH):
            each_piece(lambda p: take(c + 1, hh, p, False))

    for j in range(1, pairs):
        row_copy(peers[j], sibling, j).wait_recv()
        row_copy(peers[j], sibling, pairs + j).start()
    for j in range(pairs):
        row_copy(far[j], sibling, 0).wait_recv()

    def sum_copy(src, hh, r2, other):
        index = ((src * A + a) * NH + hh) * R + r2
        return pltpu.make_async_remote_copy(
            src_ref=send.at[src, hh, r2],
            dst_ref=recv_sum.at[src, a, hh, r2],
            send_sem=sum_send.at[((src * A + other) * NH + hh) * R + r2],
            recv_sem=sum_recv.at[index],
            device_id={"row": r, "col": c, "aux": other},
            device_id_type=MESH,
        )

    def turn_copy(src, hh, r2):
        return pltpu.make_async_remote_copy(
            src_ref=send_turn.at[src, hh, r2],
            dst_ref=recv_turn.at[c % NT, r, hh],
            send_sem=turn_send.at[(src * NH + hh) * R + r2],
            recv_sem=turn_recv.at[((c % NT) * R + r) * NH + hh],
            device_id={"row": r2, "col": src, "aux": a},
            device_id_type=MESH,
        )

    def needs(src, turned, plane):
        keeps = src // NT == plane
        return keeps | (c // NT == plane) if turned else keeps

    def each_other(src, turned, act):
        def one(k, _):
            other = (a + k) % A

            @pl.when(needs(src, turned, other))
            def _():
                act(other)

            return 0

        lax.fori_loop(1, A, one, 0)

    def share(src, hh, r2, turned):
        send[src, hh, r2] = kept[src, hh, r2].astype(jnp.bfloat16)
        each_other(src, turned, lambda other: sum_copy(src, hh, r2, other).start())

    def whole(src, turned):
        def one(r2, _):
            tile = jnp.concatenate([panel[src, hh] for hh in range(NH)], axis=1)
            value = jnp.dot(column[r2], tile, preferred_element_type=jnp.float32)
            for hh in range(NH):
                kept[src, hh, r2] = value[:, hh * LANES : (hh + 1) * LANES]
                share(src, hh, r2, turned)
            return 0

        lax.fori_loop(0, R, one, 0)

    def streamed(src, hh, up, taken=0):
        def piece(p, _):
            @pl.when(p >= taken)
            def _():
                take(src, hh, p, up)

            rows = pl.ds(pl.multiple_of(p * step, step), step)
            for r2 in range(R):
                value = jnp.dot(
                    column[r2, :, rows],
                    panel[src, hh, rows, :],
                    preferred_element_type=jnp.float32,
                )
                kept[src, hh, r2] = jnp.where(p == 0, value, kept[src, hh, r2] + value)
            return 0

        lax.fori_loop(0, PIECES, piece, 0)
        lax.fori_loop(0, R, lambda r2, _: (share(src, hh, r2, True), 0)[1], 0)

    def settle(src, hh, turned):
        @pl.when(needs(src, turned, a))
        def _():
            def one(r2, _):
                def add(k, total):
                    other = (a + k) % A
                    pltpu.make_async_remote_copy(
                        src_ref=recv_sum.at[src, other, hh, r2],
                        dst_ref=recv_sum.at[src, other, hh, r2],
                        send_sem=sum_send.at[0],
                        recv_sem=sum_recv.at[((src * A + other) * NH + hh) * R + r2],
                        device_id={"row": r, "col": c, "aux": other},
                        device_id_type=MESH,
                    ).wait_recv()
                    return total + recv_sum[src, other, hh, r2].astype(jnp.float32)

                total = lax.fori_loop(1, A, add, kept[src, hh, r2])
                kept[src, hh, r2] = total
                if turned:

                    @pl.when(c // NT == a)
                    def _():
                        send_turn[src, hh, r2] = total.astype(jnp.bfloat16)
                        turn_copy(src, hh, r2).start()

                return 0

            lax.fori_loop(0, R, one, 0)

    def settle_whole(src, turned):
        for hh in range(NH):
            settle(src, hh, turned)

    def ahead(p):
        if C > 2:

            @pl.when(has_up(c - 2))
            def _():
                take(c - 2, 0, p, True)

    whole(c, False)
    ahead(0)

    @pl.when(has_up(c - 1))
    def _():
        whole(c - 1, True)

    ahead(1)

    @pl.when(has_down(c + 1))
    def _():
        @pl.when(jnp.logical_not(passes_down))
        def _():
            for hh in range(NH):
                each_piece(lambda p: z_copy(c + 1, hh, p, False).wait_recv())

        whole(c + 1, True)

    ahead(2)

    @pl.when(has_up(c - 1))
    def _():
        settle_whole(c - 1, True)

    ahead(3)
    settle_whole(c, False)

    @pl.when(has_down(c + 1))
    def _():
        settle_whole(c + 1, True)

    steps = [(d, hh, up) for d in range(2, C) for hh in range(NH) for up in (True, False)]

    def at_step(d, up, act):
        src = c - d if up else c + d

        @pl.when(has_up(src) if up else has_down(src))
        def _():
            act(src)

    for n, (d, hh, up) in enumerate(steps):
        early = 4 if d == 2 and hh == 0 and up else 0
        at_step(d, up, lambda src: streamed(src, hh, up, early))
        if n >= 2:
            d0, hh0, up0 = steps[n - 2]
            at_step(d0, up0, lambda src: settle(src, hh0, True))
    for d0, hh0, up0 in steps[-2:]:
        at_step(d0, up0, lambda src: settle(src, hh0, True))

    for t in range(NT):
        tile = a * NT + t
        here = (tile == c) | ((tile < c) & (tile < half_c)) | ((tile > c) & (c >= half_c))

        @pl.when(here)
        def _():
            for hh in range(NH):
                for r2 in range(R):
                    out_ref[
                        t * T + hh * LANES : t * T + (hh + 1) * LANES, r2 * T : (r2 + 1) * T
                    ] = kept[tile, hh, r2].T

        @pl.when(jnp.logical_not(here))
        def _():
            for hh in range(NH):
                for r2 in range(R):
                    pltpu.make_async_remote_copy(
                        src_ref=recv_turn.at[t, r2, hh],
                        dst_ref=recv_turn.at[t, r2, hh],
                        send_sem=turn_send.at[0],
                        recv_sem=turn_recv.at[(t * R + r2) * NH + hh],
                        device_id={"row": r2, "col": (c + 1) % C, "aux": a},
                        device_id_type=MESH,
                    ).wait_recv()
                    out_ref[
                        t * T : (t + 1) * T, r2 * T + hh * LANES : r2 * T + (hh + 1) * LANES
                    ] = recv_turn[t, r2, hh].astype(jnp.float32)

    for j in range(1, pairs):
        row_copy(r, peers[j], j).wait_send()
        row_copy(peers[j], sibling, pairs + j).wait_send()
    row_copy(r, sibling, 0).wait_send()
    for hh in range(NH):

        @pl.when(sends_up)
        def _():
            each_piece(lambda p: z_copy(c, hh, p, True).wait_send())

        @pl.when(sends_down)
        def _():
            each_piece(lambda p: z_copy(c, hh, p, False).wait_send())

    def finish(src, hh, up, turned):
        def every_row(act):
            lax.fori_loop(0, R, lambda r2, _: (act(r2), 0)[1], 0)

        if turned:

            @pl.when((c + 1 < C) if up else (c - 1 >= half_c))
            def _():
                each_piece(lambda p: z_copy(src, hh, p, up).wait_send())

            @pl.when(c // NT == a)
            def _():
                every_row(lambda r2: turn_copy(src, hh, r2).wait_send())

        each_other(
            src,
            turned,
            lambda other: every_row(lambda r2: sum_copy(src, hh, r2, other).wait_send()),
        )

    for hh in range(NH):
        finish(c, hh, True, False)
    for d in range(1, C):
        for hh in range(NH):

            @pl.when(has_up(c - d))
            def _():
                finish(c - d, hh, True, True)

            @pl.when(has_down(c + d))
            def _():
                finish(c + d, hh, False, True)


def local(sizes, integrals, block_mask, block_slots, orbitals):
    R, C, A = sizes
    _, cap, blk, width = integrals.shape
    mb = block_mask.shape[1]
    occ = orbitals.shape[0]
    T = mb * blk
    kdim = occ * (width // blk)
    NH, NT, pieces = T // LANES, C // A, 6
    dims = (R, C, A, mb, occ, blk, cap, kdim, pieces)
    dma = pltpu.SemaphoreType.DMA
    bf16, f32 = jnp.bfloat16, jnp.float32
    vmem = pl.BlockSpec(memory_space=pltpu.VMEM)
    weights = pl.pallas_call(
        functools.partial(weigh, (mb, occ, blk, cap)),
        out_shape=jax.ShapeDtypeStruct((mb * occ, cap * blk), bf16),
        in_specs=[vmem] * 3,
        out_specs=vmem,
    )(
        block_mask.reshape(block_mask.shape[1:]),
        block_slots.reshape(block_slots.shape[1:]),
        orbitals,
    )
    result = pl.pallas_call(
        functools.partial(kernel, dims),
        out_shape=jax.ShapeDtypeStruct((NT * T, R * T), f32),
        in_specs=[pl.BlockSpec(memory_space=pl.ANY), vmem],
        out_specs=vmem,
        scratch_shapes=[
            pltpu.VMEM((cap * blk, width), bf16),
            pltpu.VMEM((C, NH, kdim, LANES), bf16),
            pltpu.VMEM((R, T, kdim), bf16),
            pltpu.VMEM((C, NH, R, T, LANES), f32),
            pltpu.VMEM((C, NH, R, T, LANES), bf16),
            pltpu.VMEM((C, A, NH, R, T, LANES), bf16),
            pltpu.VMEM((C, NH, R, T, LANES), bf16),
            pltpu.VMEM((NT, R, NH, T, LANES), bf16),
            dma(()),
            dma((C * NH * pieces,)),
            dma((C * NH * pieces,)),
            dma((C * NH * pieces,)),
            dma((R,)),
            dma((R,)),
            dma((C * A * NH * R,)),
            dma((C * A * NH * R,)),
            dma((C * NH * R,)),
            dma((NT * R * NH,)),
        ],
        compiler_params=pltpu.CompilerParams(
            collective_id=0, has_side_effects=True, vmem_limit_bytes=60 * 1024 * 1024
        ),
        cost_estimate=pl.CostEstimate(
            flops=2 * C * T * R * T * kdim, bytes_accessed=8 * 1024 * 1024, transcendentals=0
        ),
    )(
        integrals.reshape(cap * blk, width),
        weights,
    )
    return result.reshape(NT * T, R, T)


def solution(mesh):
    sizes = tuple(mesh.shape[name] for name in ("row", "col", "aux"))
    placed = (
        P("aux", ("row", "col"), None, None),
        P("aux", ("row", "col"), None),
        P("aux", ("row", "col"), None),
        P(),
    )
    return jax.shard_map(
        functools.partial(local, sizes),
        mesh=mesh,
        in_specs=placed,
        out_specs=P(("row", "aux"), None, "col"),
        check_vma=False,
    )
```

```python
import functools

import jax
import jax.numpy as jnp
from jax import lax
from jax.experimental import pallas as pl
from jax.experimental.pallas import tpu as pltpu
from jax.sharding import PartitionSpec as P

MESH = pl.DeviceIdType.MESH
LANES = 128


def weigh(dims, mask_ref, slot_ref, orb_ref, weights):
    MB, OCC, BLK, CAP = dims
    mask, slot = mask_ref[...], slot_ref[...]
    lane_count = mask.shape[1]
    row_ids = lax.broadcasted_iota(jnp.int32, mask.shape, 0)
    lam_ids = lax.broadcasted_iota(jnp.int32, mask.shape, 1)
    code = row_ids * lane_count + lam_ids
    low = lax.broadcasted_iota(jnp.int32, (OCC, LANES), 1) < BLK

    def slot_block(s, half):
        select = jnp.where((mask == 1) & (slot == s), 1, 0)
        position = jnp.sum(select * (code + 1))
        present = jnp.minimum(position, 1)
        place = jnp.maximum(position - 1, 0)
        lam, row = place % lane_count, place // lane_count
        start = pl.multiple_of((lam // 2) * LANES, LANES)
        values = orb_ref[:, pl.ds(start, LANES)].astype(jnp.float32)
        odd = lam % 2
        values = jnp.where(odd == half, values, pltpu.roll(values, BLK, 1))
        return values, row, present

    for p in range(CAP // 2):
        lo, lo_row, lo_here = slot_block(2 * p, 0)
        hi, hi_row, hi_here = slot_block(2 * p + 1, 1)
        for b in range(MB):
            lo_w = jnp.where(lo_row == b, lo_here, 0).astype(jnp.float32)
            hi_w = jnp.where(hi_row == b, hi_here, 0).astype(jnp.float32)
            weights[b * OCC : (b + 1) * OCC, p * LANES : (p + 1) * LANES] = jnp.where(
                low, lo * lo_w, hi * hi_w
            ).astype(jnp.bfloat16)


def kernel(
    dims,
    packed_hbm,
    weights,
    out_ref,
    packed_ref,
    panel,
    column,
    block,
    kept,
    send,
    recv_sum,
    recv_turn,
    load,
    z_recv,
    z_up,
    z_down,
    row_recv,
    row_send,
    sum_send,
    sum_recv,
    turn_send,
    turn_recv,
):
    R, C, A, MB, OCC, BLK, CAP, KDIM, PIECES = dims
    T = MB * BLK
    NH = T // LANES
    NT = C // A
    half_c = C // 2
    step = KDIM // PIECES
    r, c, a = lax.axis_index("row"), lax.axis_index("col"), lax.axis_index("aux")
    devices = R * C * A
    me = (r * C + c) * A + a

    loading = pltpu.make_async_copy(packed_hbm, packed_ref, load)
    loading.start()
    barrier = pltpu.get_barrier_semaphore()

    def greet(k, _):
        @pl.when(k != me)
        def _():
            pl.semaphore_signal(
                barrier,
                inc=1,
                device_id={"row": k // (C * A), "col": (k // A) % C, "aux": k % A},
                device_id_type=MESH,
            )

        return 0

    lax.fori_loop(0, devices, greet, 0)

    low = lax.broadcasted_iota(jnp.int32, (OCC, LANES), 1) < BLK

    def transform(g, _):
        at = pl.multiple_of(g * 256, 256)
        h = jnp.dot(
            weights[...], packed_ref[:, pl.ds(at, 256)], preferred_element_type=jnp.float32
        )
        for hh in range(NH):
            parts = []
            for j in range(2):
                b0 = h[2 * hh * OCC : (2 * hh + 1) * OCC, j * LANES : (j + 1) * LANES]
                b1 = h[(2 * hh + 1) * OCC : (2 * hh + 2) * OCC, j * LANES : (j + 1) * LANES]
                parts.append(jnp.where(low, b0, pltpu.roll(b1, BLK, 1)))
                parts.append(jnp.where(low, pltpu.roll(b0, BLK, 1), b1))
            tile = jnp.concatenate(parts, axis=0)
            panel[c, hh, pl.ds(at, 256), :] = tile.astype(jnp.bfloat16)
            column[r, hh * LANES : (hh + 1) * LANES, pl.ds(at, 256)] = tile.T.astype(jnp.bfloat16)
        return 0

    def z_copy(src, hh, p, up):
        ref = panel.at[src, hh, pl.ds(pl.multiple_of(p * step, step), step), :]
        target = jnp.minimum(c + 1, C - 1) if up else jnp.maximum(c - 1, 0)
        index = (src * NH + hh) * PIECES + p
        return pltpu.make_async_remote_copy(
            src_ref=ref,
            dst_ref=ref,
            send_sem=(z_up if up else z_down).at[index],
            recv_sem=z_recv.at[index],
            device_id={"row": r, "col": target, "aux": a},
            device_id_type=MESH,
        )

    def row_copy(tile, target, send_index, p):
        ref = column.at[tile, :, pl.ds(pl.multiple_of(p * step, step), step)]
        return pltpu.make_async_remote_copy(
            src_ref=ref,
            dst_ref=ref,
            send_sem=row_send.at[send_index * PIECES + p],
            recv_sem=row_recv.at[tile * PIECES + p],
            device_id={"row": target, "col": c, "aux": a},
            device_id_type=MESH,
        )

    def each_piece(act):
        lax.fori_loop(0, PIECES, lambda p, _: (act(p), 0)[1], 0)

    sends_up = (c < half_c) & (c + 1 < C)
    sends_down = c - 1 >= half_c
    sibling = r + 1 - 2 * (r % 2)
    pairs = R // 2
    peers = [(r + 2 * j) % R for j in range(pairs)]
    far = [(sibling + 2 * j) % R for j in range(pairs)]

    def send_own(hh, p):
        @pl.when(sends_up)
        def _():
            z_copy(c, hh, p, True).start()

        @pl.when(sends_down)
        def _():
            z_copy(c, hh, p, False).start()

    edge = half_c - 1
    loading.wait()
    pl.semaphore_wait(barrier, devices - 1)

    def make_piece(p, _):
        lax.fori_loop(p * (step // 256), (p + 1) * (step // 256), transform, 0)
        for j in range(1, pairs):
            row_copy(r, peers[j], j, p).start()
        send_own(0, p)

        @pl.when(c == edge)
        def _():
            for hh in range(1, NH):
                send_own(hh, p)

        row_copy(r, sibling, 0, p).start()
        return 0

    lax.fori_loop(0, PIECES, make_piece, 0)

    @pl.when(c != edge)
    def _():
        for hh in range(1, NH):
            each_piece(lambda p: send_own(hh, p))

    def has_up(src):
        return (src >= 0) & (src < half_c)

    def has_down(src):
        return (src < C) & (c >= half_c)

    def take(src, hh, p, up):
        z_copy(src, hh, p, up).wait_recv()

        @pl.when((c + 1 < C) if up else (c - 1 >= half_c))
        def _():
            z_copy(src, hh, p, up).start()

    passes_down = c - 1 >= half_c

    @pl.when(has_up(c - 1))
    def _():
        def one(n, _):
            by_piece = c - 1 == edge
            hh = jnp.where(by_piece, n % NH, n // PIECES)
            p = jnp.where(by_piece, n // NH, n % PIECES)
            take(c - 1, hh, p, True)
            return 0

        lax.fori_loop(0, NH * PIECES, one, 0)

    @pl.when(has_down(c + 1) & passes_down)
    def _():
        for hh in range(NH):
            each_piece(lambda p: take(c + 1, hh, p, False))

    def pass_row(j, p):
        row_copy(peers[j], sibling, j, p).wait_recv()
        row_copy(peers[j], sibling, pairs + j, p).start()

    for j in range(1, pairs):
        each_piece(lambda p: pass_row(j, p))
    for j in range(pairs):
        each_piece(lambda p: row_copy(far[j], sibling, 0, p).wait_recv())

    def sum_copy(src, hh):
        return pltpu.make_async_remote_copy(
            src_ref=send.at[src, hh],
            dst_ref=recv_sum.at[src % NT, a, hh],
            send_sem=sum_send.at[src * NH + hh],
            recv_sem=sum_recv.at[((src % NT) * A + a) * NH + hh],
            device_id={"row": r, "col": c, "aux": src // NT},
            device_id_type=MESH,
        )

    def turn_copy(src, hh, r2):
        return pltpu.make_async_remote_copy(
            src_ref=send.at[src, hh, r2],
            dst_ref=recv_turn.at[c % NT, a, r, hh],
            send_sem=turn_send.at[(src * NH + hh) * R + r2],
            recv_sem=turn_recv.at[(((c % NT) * A + a) * R + r) * NH + hh],
            device_id={"row": r2, "col": src, "aux": c // NT},
            device_id_type=MESH,
        )

    def settle(src, hh, r2, value, turned):
        send[src, hh, r2] = value.astype(jnp.bfloat16)
        if turned:
            turn_copy(src, hh, r2).start()

        @pl.when(src // NT == a)
        def _():
            kept[src % NT, hh, r2] = value

    def pass_sum(src, hh):
        @pl.when(src // NT != a)
        def _():
            sum_copy(src, hh).start()

    def whole(src, turned):
        def one(r2, _):
            tile = jnp.concatenate([panel[src, hh] for hh in range(NH)], axis=1)
            value = jnp.dot(column[r2], tile, preferred_element_type=jnp.float32)
            for hh in range(NH):
                settle(src, hh, r2, value[:, hh * LANES : (hh + 1) * LANES], turned)
            return 0

        lax.fori_loop(0, R, one, 0)
        for hh in range(NH):
            pass_sum(src, hh)

    def streamed(src, hh, up, taken):
        def piece(p, _):
            @pl.when(p >= taken)
            def _():
                take(src, hh, p, up)

            rows = pl.ds(pl.multiple_of(p * step, step), step)
            for r2 in range(R):
                value = jnp.dot(
                    column[r2, :, rows],
                    panel[src, hh, rows, :],
                    preferred_element_type=jnp.float32,
                )
                block[r2] = jnp.where(p == 0, value, block[r2] + value)
            return 0

        lax.fori_loop(0, PIECES, piece, 0)

        def one(r2, _):
            settle(src, hh, r2, block[r2], True)
            return 0

        lax.fori_loop(0, R, one, 0)
        pass_sum(src, hh)

    def ahead(p):
        if C > 2:

            @pl.when(has_up(c - 2))
            def _():
                take(c - 2, 0, p, True)

    block[...] = jnp.zeros_like(block)
    ahead(0)
    whole(c, False)
    ahead(1)

    @pl.when(has_up(c - 1))
    def _():
        whole(c - 1, True)

    ahead(2)

    def nearest_down():
        @pl.when(has_down(c + 1))
        def _():
            @pl.when(jnp.logical_not(passes_down))
            def _():
                for hh in range(NH):
                    each_piece(lambda p: z_copy(c + 1, hh, p, False).wait_recv())

            whole(c + 1, True)

    for d in range(2, C):
        for hh in range(NH):

            @pl.when(has_up(c - d))
            def _():
                streamed(c - d, hh, True, 3 if d == 2 and hh == 0 else 0)

            if d == 2 and hh == 0:
                nearest_down()

            @pl.when(has_down(c + d))
            def _():
                streamed(c + d, hh, False, 0)

    if C == 2:
        nearest_down()

    for t in range(NT):
        tile = a * NT + t
        here = (tile == c) | ((tile < c) & (tile < half_c)) | ((tile > c) & (c >= half_c))

        @pl.when(here)
        def _():
            for hh in range(NH):

                def arrived(other, _):
                    source = (a + other) % A
                    index = (t * A + source) * NH + hh
                    pltpu.make_async_remote_copy(
                        src_ref=recv_sum.at[t, source, hh],
                        dst_ref=recv_sum.at[t, source, hh],
                        send_sem=sum_send.at[0],
                        recv_sem=sum_recv.at[index],
                        device_id={"row": r, "col": c, "aux": source},
                        device_id_type=MESH,
                    ).wait_recv()
                    kept[t, hh] = kept[t, hh] + recv_sum[t, source, hh].astype(jnp.float32)
                    return 0

                lax.fori_loop(1, A, arrived, 0)
                for r2 in range(R):
                    out_ref[
                        t * T + hh * LANES : t * T + (hh + 1) * LANES, r2 * T : (r2 + 1) * T
                    ] = kept[t, hh, r2].T

        @pl.when(jnp.logical_not(here))
        def _():
            for hh in range(NH):
                for r2 in range(R):

                    def add(source, total):
                        index = ((t * A + source) * R + r2) * NH + hh
                        pltpu.make_async_remote_copy(
                            src_ref=recv_turn.at[t, source, r2, hh],
                            dst_ref=recv_turn.at[t, source, r2, hh],
                            send_sem=turn_send.at[0],
                            recv_sem=turn_recv.at[index],
                            device_id={"row": r2, "col": tile, "aux": source},
                            device_id_type=MESH,
                        ).wait_recv()
                        return total + recv_turn[t, source, r2, hh].astype(jnp.float32)

                    out_ref[
                        t * T : (t + 1) * T, r2 * T + hh * LANES : r2 * T + (hh + 1) * LANES
                    ] = lax.fori_loop(0, A, add, jnp.zeros((T, LANES), jnp.float32))

    def row_sent(p):
        for j in range(1, pairs):
            row_copy(r, peers[j], j, p).wait_send()
            row_copy(peers[j], sibling, pairs + j, p).wait_send()
        row_copy(r, sibling, 0, p).wait_send()

    each_piece(row_sent)
    for hh in range(NH):

        @pl.when(sends_up)
        def _():
            each_piece(lambda p: z_copy(c, hh, p, True).wait_send())

        @pl.when(sends_down)
        def _():
            each_piece(lambda p: z_copy(c, hh, p, False).wait_send())

    def finish(src, hh, up, turned):
        if turned:

            @pl.when((c + 1 < C) if up else (c - 1 >= half_c))
            def _():
                each_piece(lambda p: z_copy(src, hh, p, up).wait_send())

            lax.fori_loop(0, R, lambda r2, _: (turn_copy(src, hh, r2).wait_send(), 0)[1], 0)

        @pl.when(src // NT != a)
        def _():
            sum_copy(src, hh).wait_send()

    for hh in range(NH):
        finish(c, hh, True, False)
    for d in range(1, C):
        for hh in range(NH):

            @pl.when(has_up(c - d))
            def _():
                finish(c - d, hh, True, True)

            @pl.when(has_down(c + d))
            def _():
                finish(c + d, hh, False, True)


def local(sizes, integrals, block_mask, block_slots, orbitals):
    R, C, A = sizes
    _, cap, blk, width = integrals.shape
    mb = block_mask.shape[1]
    occ = orbitals.shape[0]
    T = mb * blk
    kdim = occ * (width // blk)
    NH, NT, pieces = T // LANES, C // A, 6
    dims = (R, C, A, mb, occ, blk, cap, kdim, pieces)
    dma = pltpu.SemaphoreType.DMA
    bf16, f32 = jnp.bfloat16, jnp.float32
    vmem = pl.BlockSpec(memory_space=pltpu.VMEM)
    weights = pl.pallas_call(
        functools.partial(weigh, (mb, occ, blk, cap)),
        out_shape=jax.ShapeDtypeStruct((mb * occ, cap * blk), bf16),
        in_specs=[vmem] * 3,
        out_specs=vmem,
    )(
        block_mask.reshape(block_mask.shape[1:]),
        block_slots.reshape(block_slots.shape[1:]),
        orbitals,
    )
    result = pl.pallas_call(
        functools.partial(kernel, dims),
        out_shape=jax.ShapeDtypeStruct((NT * T, R * T), f32),
        in_specs=[pl.BlockSpec(memory_space=pl.ANY), vmem],
        out_specs=vmem,
        scratch_shapes=[
            pltpu.VMEM((cap * blk, width), bf16),
            pltpu.VMEM((C, NH, kdim, LANES), bf16),
            pltpu.VMEM((R, T, kdim), bf16),
            pltpu.VMEM((R, T, LANES), f32),
            pltpu.VMEM((NT, NH, R, T, LANES), f32),
            pltpu.VMEM((C, NH, R, T, LANES), bf16),
            pltpu.VMEM((NT, A, NH, R, T, LANES), bf16),
            pltpu.VMEM((NT, A, R, NH, T, LANES), bf16),
            dma(()),
            dma((C * NH * pieces,)),
            dma((C * NH * pieces,)),
            dma((C * NH * pieces,)),
            dma((R * pieces,)),
            dma((R * pieces,)),
            dma((C * NH,)),
            dma((NT * A * NH,)),
            dma((C * NH * R,)),
            dma((NT * A * R * NH,)),
        ],
        compiler_params=pltpu.CompilerParams(
            collective_id=0, has_side_effects=True, vmem_limit_bytes=50 * 1024 * 1024
        ),
        cost_estimate=pl.CostEstimate(
            flops=2 * C * T * R * T * kdim, bytes_accessed=8 * 1024 * 1024, transcendentals=0
        ),
    )(
        integrals.reshape(cap * blk, width),
        weights,
    )
    return result.reshape(NT * T, R, T)


def solution(mesh):
    sizes = tuple(mesh.shape[name] for name in ("row", "col", "aux"))
    placed = (
        P("aux", ("row", "col"), None, None),
        P("aux", ("row", "col"), None),
        P("aux", ("row", "col"), None),
        P(),
    )
    return jax.shard_map(
        functools.partial(local, sizes),
        mesh=mesh,
        in_specs=placed,
        out_specs=P(("row", "aux"), None, "col"),
        check_vma=False,
    )
```

```python
import functools

import jax
import jax.numpy as jnp
from jax import lax
from jax.experimental import pallas as pl
from jax.experimental.pallas import tpu as pltpu
from jax.sharding import PartitionSpec as P

MESH = pl.DeviceIdType.MESH
LANES = 128


def weigh(dims, mask_ref, slot_ref, orb_ref, weights):
    MB, OCC, BLK, CAP = dims
    mask, slot = mask_ref[...], slot_ref[...]
    lane_count = mask.shape[1]
    row_ids = lax.broadcasted_iota(jnp.int32, mask.shape, 0)
    lam_ids = lax.broadcasted_iota(jnp.int32, mask.shape, 1)
    code = row_ids * lane_count + lam_ids
    low = lax.broadcasted_iota(jnp.int32, (OCC, LANES), 1) < BLK

    def slot_block(s, half):
        select = jnp.where((mask == 1) & (slot == s), 1, 0)
        position = jnp.sum(select * (code + 1))
        present = jnp.minimum(position, 1)
        place = jnp.maximum(position - 1, 0)
        lam, row = place % lane_count, place // lane_count
        start = pl.multiple_of((lam // 2) * LANES, LANES)
        values = orb_ref[:, pl.ds(start, LANES)].astype(jnp.float32)
        odd = lam % 2
        values = jnp.where(odd == half, values, pltpu.roll(values, BLK, 1))
        return values, row, present

    for p in range(CAP // 2):
        lo, lo_row, lo_here = slot_block(2 * p, 0)
        hi, hi_row, hi_here = slot_block(2 * p + 1, 1)
        for b in range(MB):
            lo_w = jnp.where(lo_row == b, lo_here, 0).astype(jnp.float32)
            hi_w = jnp.where(hi_row == b, hi_here, 0).astype(jnp.float32)
            weights[b * OCC : (b + 1) * OCC, p * LANES : (p + 1) * LANES] = jnp.where(
                low, lo * lo_w, hi * hi_w
            ).astype(jnp.bfloat16)


def row_parts(T):
    return [(0, T // 2), (T // 2, T // 4), (3 * T // 4, T // 4)]


def kernel(
    dims,
    packed_hbm,
    weights,
    out_ref,
    packed_ref,
    panel,
    column,
    block,
    kept,
    send,
    recv_sum,
    recv_turn,
    load,
    z_recv,
    z_up,
    z_down,
    row_recv,
    row_send,
    sum_send,
    sum_recv,
    turn_send,
    turn_recv,
):
    R, C, A, MB, OCC, BLK, CAP, KDIM, PIECES = dims
    T = MB * BLK
    parts = row_parts(T)
    NH = len(parts)
    NT = C // A
    half_c = C // 2
    step = KDIM // PIECES
    r, c, a = lax.axis_index("row"), lax.axis_index("col"), lax.axis_index("aux")
    devices = R * C * A
    me = (r * C + c) * A + a

    loading = pltpu.make_async_copy(packed_hbm, packed_ref, load)
    loading.start()
    barrier = pltpu.get_barrier_semaphore()

    def greet(k, _):
        @pl.when(k != me)
        def _():
            pl.semaphore_signal(
                barrier,
                inc=1,
                device_id={"row": k // (C * A), "col": (k // A) % C, "aux": k % A},
                device_id_type=MESH,
            )

        return 0

    lax.fori_loop(0, devices, greet, 0)

    low = lax.broadcasted_iota(jnp.int32, (OCC, LANES), 1) < BLK

    def transform(g, _):
        at = pl.multiple_of(g * 256, 256)
        h = jnp.dot(
            weights[...], packed_ref[:, pl.ds(at, 256)], preferred_element_type=jnp.float32
        )
        for hh in range(T // LANES):
            quarters = []
            for j in range(2):
                b0 = h[2 * hh * OCC : (2 * hh + 1) * OCC, j * LANES : (j + 1) * LANES]
                b1 = h[(2 * hh + 1) * OCC : (2 * hh + 2) * OCC, j * LANES : (j + 1) * LANES]
                quarters.append(jnp.where(low, b0, pltpu.roll(b1, BLK, 1)))
                quarters.append(jnp.where(low, pltpu.roll(b0, BLK, 1), b1))
            tile = jnp.concatenate(quarters, axis=0)
            column[r, hh * LANES : (hh + 1) * LANES, pl.ds(at, 256)] = tile.T.astype(jnp.bfloat16)
        return 0

    def z_copy(src, hh, p, up, own=False):
        start, size = parts[hh]
        lanes = pl.ds(pl.multiple_of(p * step, step), step)
        ref = panel.at[src, pl.ds(start, size), lanes]
        target = jnp.minimum(c + 1, C - 1) if up else jnp.maximum(c - 1, 0)
        index = (src * NH + hh) * PIECES + p
        return pltpu.make_async_remote_copy(
            src_ref=column.at[r, pl.ds(start, size), lanes] if own else ref,
            dst_ref=ref,
            send_sem=(z_up if up else z_down).at[index],
            recv_sem=z_recv.at[index],
            device_id={"row": r, "col": target, "aux": a},
            device_id_type=MESH,
        )

    def row_copy(tile, target, send_index, p):
        ref = column.at[tile, :, pl.ds(pl.multiple_of(p * step, step), step)]
        return pltpu.make_async_remote_copy(
            src_ref=ref,
            dst_ref=ref,
            send_sem=row_send.at[send_index * PIECES + p],
            recv_sem=row_recv.at[tile * PIECES + p],
            device_id={"row": target, "col": c, "aux": a},
            device_id_type=MESH,
        )

    def each_piece(act):
        lax.fori_loop(0, PIECES, lambda p, _: (act(p), 0)[1], 0)

    sends_up = (c < half_c) & (c + 1 < C)
    sends_down = c - 1 >= half_c
    sibling = r + 1 - 2 * (r % 2)
    pairs = R // 2
    peers = [(r + 2 * j) % R for j in range(pairs)]
    far = [(sibling + 2 * j) % R for j in range(pairs)]

    def send_own(hh, p):
        @pl.when(sends_up)
        def _():
            z_copy(c, hh, p, True, True).start()

        @pl.when(sends_down)
        def _():
            z_copy(c, hh, p, False, True).start()

    edge = half_c - 1
    loading.wait()
    pl.semaphore_wait(barrier, devices - 1)

    def make_piece(p, _):
        lax.fori_loop(p * (step // 256), (p + 1) * (step // 256), transform, 0)
        for j in range(1, pairs):
            row_copy(r, peers[j], j, p).start()
        send_own(0, p)

        @pl.when(c == edge)
        def _():
            for hh in range(1, NH):
                send_own(hh, p)

        row_copy(r, sibling, 0, p).start()
        return 0

    lax.fori_loop(0, PIECES, make_piece, 0)

    @pl.when(c != edge)
    def _():
        for hh in range(1, NH):
            each_piece(lambda p: send_own(hh, p))

    def has_up(src):
        return (src >= 0) & (src < half_c)

    def has_down(src):
        return (src < C) & (c >= half_c)

    def take(src, hh, p, up):
        z_copy(src, hh, p, up).wait_recv()

        @pl.when((c + 1 < C) if up else (c - 1 >= half_c))
        def _():
            z_copy(src, hh, p, up).start()

    passes_down = c - 1 >= half_c

    @pl.when(has_up(c - 1) & (c - 1 == edge))
    def _():
        def every_part(p):
            for hh in range(NH):
                take(c - 1, hh, p, True)

        each_piece(every_part)

    @pl.when(has_up(c - 1) & (c - 1 != edge))
    def _():
        for hh in range(NH):
            each_piece(lambda p: take(c - 1, hh, p, True))

    @pl.when(has_down(c + 1) & passes_down)
    def _():
        for hh in range(NH):
            each_piece(lambda p: take(c + 1, hh, p, False))

    def pass_row(j, p):
        row_copy(peers[j], sibling, j, p).wait_recv()
        row_copy(peers[j], sibling, pairs + j, p).start()

    for j in range(1, pairs):
        each_piece(lambda p: pass_row(j, p))
    for j in range(pairs):
        each_piece(lambda p: row_copy(far[j], sibling, 0, p).wait_recv())

    def sum_copy(src, hh):
        rows = pl.ds(*parts[hh])
        return pltpu.make_async_remote_copy(
            src_ref=send.at[src, :, rows],
            dst_ref=recv_sum.at[src % NT, a, :, rows],
            send_sem=sum_send.at[src * NH + hh],
            recv_sem=sum_recv.at[((src % NT) * A + a) * NH + hh],
            device_id={"row": r, "col": c, "aux": src // NT},
            device_id_type=MESH,
        )

    def turn_copy(src, hh, r2):
        rows = pl.ds(*parts[hh])
        return pltpu.make_async_remote_copy(
            src_ref=send.at[src, r2, rows],
            dst_ref=recv_turn.at[c % NT, a, r, rows],
            send_sem=turn_send.at[(src * NH + hh) * R + r2],
            recv_sem=turn_recv.at[(((c % NT) * A + a) * R + r) * NH + hh],
            device_id={"row": r2, "col": src, "aux": c // NT},
            device_id_type=MESH,
        )

    def settle(src, hh, r2, value, turned):
        rows = pl.ds(*parts[hh])
        send[src, r2, rows] = value.astype(jnp.bfloat16)
        if turned:
            turn_copy(src, hh, r2).start()

        @pl.when(src // NT == a)
        def _():
            kept[src % NT, r2, rows] = value

    def pass_sum(src, hh):
        @pl.when(src // NT != a)
        def _():
            sum_copy(src, hh).start()

    def across(left, right):
        return lax.dot_general(
            left, right, (((1,), (1,)), ((), ())), preferred_element_type=jnp.float32
        )

    def whole(src, turned):
        def one(r2, _):
            value = across(panel[src] if turned else column[r], column[r2])
            for hh, (start, size) in enumerate(parts):
                settle(src, hh, r2, value[start : start + size], turned)
            return 0

        lax.fori_loop(0, R, one, 0)
        for hh in range(NH):
            pass_sum(src, hh)

    def streamed(src, hh, up, taken):
        start, size = parts[hh]

        def piece(p, _):
            @pl.when(p >= taken)
            def _():
                take(src, hh, p, up)

            lanes = pl.ds(pl.multiple_of(p * step, step), step)
            for r2 in range(R):
                value = across(column[r2, :, lanes], panel[src, pl.ds(start, size), lanes])
                old = block[r2, :, :size]
                block[r2, :, :size] = jnp.where(p == 0, value, old + value)
            return 0

        lax.fori_loop(0, PIECES, piece, 0)

        def one(r2, _):
            settle(src, hh, r2, block[r2].T[:size], True)
            return 0

        lax.fori_loop(0, R, one, 0)
        pass_sum(src, hh)

    def ahead(p):
        if C > 2:

            @pl.when(has_up(c - 2))
            def _():
                take(c - 2, 0, p, True)

    block[...] = jnp.zeros_like(block)
    ahead(0)
    whole(c, False)
    ahead(1)

    @pl.when(has_up(c - 1))
    def _():
        whole(c - 1, True)

    ahead(2)

    def nearest_down():
        @pl.when(has_down(c + 1))
        def _():
            @pl.when(jnp.logical_not(passes_down))
            def _():
                for hh in range(NH):
                    each_piece(lambda p: z_copy(c + 1, hh, p, False).wait_recv())

            whole(c + 1, True)

    for d in range(2, C):
        for hh in range(NH):

            @pl.when(has_up(c - d))
            def _():
                streamed(c - d, hh, True, 3 if d == 2 and hh == 0 else 0)

            if d == 2 and hh == 0:
                nearest_down()

            @pl.when(has_down(c + d))
            def _():
                streamed(c + d, hh, False, 0)

    if C == 2:
        nearest_down()

    for t in range(NT):
        tile = a * NT + t
        here = (tile == c) | ((tile < c) & (tile < half_c)) | ((tile > c) & (c >= half_c))

        @pl.when(here)
        def _():
            for hh in range(NH):
                rows = pl.ds(*parts[hh])

                def arrived(other, _):
                    source = (a + other) % A
                    index = (t * A + source) * NH + hh
                    pltpu.make_async_remote_copy(
                        src_ref=recv_sum.at[t, source, :, rows],
                        dst_ref=recv_sum.at[t, source, :, rows],
                        send_sem=sum_send.at[0],
                        recv_sem=sum_recv.at[index],
                        device_id={"row": r, "col": c, "aux": source},
                        device_id_type=MESH,
                    ).wait_recv()
                    kept[t, :, rows] = kept[t, :, rows] + recv_sum[t, source, :, rows].astype(
                        jnp.float32
                    )
                    return 0

                lax.fori_loop(1, A, arrived, 0)
            for r2 in range(R):
                out_ref[t * T : (t + 1) * T, r2 * T : (r2 + 1) * T] = kept[t, r2]

        @pl.when(jnp.logical_not(here))
        def _():
            for r2 in range(R):

                def add(source, total):
                    for hh in range(NH):
                        rows = pl.ds(*parts[hh])
                        index = ((t * A + source) * R + r2) * NH + hh
                        pltpu.make_async_remote_copy(
                            src_ref=recv_turn.at[t, source, r2, rows],
                            dst_ref=recv_turn.at[t, source, r2, rows],
                            send_sem=turn_send.at[0],
                            recv_sem=turn_recv.at[index],
                            device_id={"row": r2, "col": tile, "aux": source},
                            device_id_type=MESH,
                        ).wait_recv()
                    return total + recv_turn[t, source, r2].astype(jnp.float32)

                total = lax.fori_loop(0, A, add, jnp.zeros((T, T), jnp.float32))
                out_ref[t * T : (t + 1) * T, r2 * T : (r2 + 1) * T] = total.T

    def row_sent(p):
        for j in range(1, pairs):
            row_copy(r, peers[j], j, p).wait_send()
            row_copy(peers[j], sibling, pairs + j, p).wait_send()
        row_copy(r, sibling, 0, p).wait_send()

    each_piece(row_sent)
    for hh in range(NH):

        @pl.when(sends_up)
        def _():
            each_piece(lambda p: z_copy(c, hh, p, True, True).wait_send())

        @pl.when(sends_down)
        def _():
            each_piece(lambda p: z_copy(c, hh, p, False, True).wait_send())

    def finish(src, hh, up, turned):
        if turned:

            @pl.when((c + 1 < C) if up else (c - 1 >= half_c))
            def _():
                each_piece(lambda p: z_copy(src, hh, p, up).wait_send())

            lax.fori_loop(0, R, lambda r2, _: (turn_copy(src, hh, r2).wait_send(), 0)[1], 0)

        @pl.when(src // NT != a)
        def _():
            sum_copy(src, hh).wait_send()

    for hh in range(NH):
        finish(c, hh, True, False)
    for d in range(1, C):
        for hh in range(NH):

            @pl.when(has_up(c - d))
            def _():
                finish(c - d, hh, True, True)

            @pl.when(has_down(c + d))
            def _():
                finish(c + d, hh, False, True)


def local(sizes, integrals, block_mask, block_slots, orbitals):
    R, C, A = sizes
    _, cap, blk, width = integrals.shape
    mb = block_mask.shape[1]
    occ = orbitals.shape[0]
    T = mb * blk
    kdim = occ * (width // blk)
    NH, NT, pieces = len(row_parts(T)), C // A, 6
    dims = (R, C, A, mb, occ, blk, cap, kdim, pieces)
    dma = pltpu.SemaphoreType.DMA
    bf16, f32 = jnp.bfloat16, jnp.float32
    vmem = pl.BlockSpec(memory_space=pltpu.VMEM)
    weights = pl.pallas_call(
        functools.partial(weigh, (mb, occ, blk, cap)),
        out_shape=jax.ShapeDtypeStruct((mb * occ, cap * blk), bf16),
        in_specs=[vmem] * 3,
        out_specs=vmem,
    )(
        block_mask.reshape(block_mask.shape[1:]),
        block_slots.reshape(block_slots.shape[1:]),
        orbitals,
    )
    result = pl.pallas_call(
        functools.partial(kernel, dims),
        out_shape=jax.ShapeDtypeStruct((NT * T, R * T), f32),
        in_specs=[pl.BlockSpec(memory_space=pl.ANY), vmem],
        out_specs=vmem,
        scratch_shapes=[
            pltpu.VMEM((cap * blk, width), bf16),
            pltpu.VMEM((C, T, kdim), bf16),
            pltpu.VMEM((R, T, kdim), bf16),
            pltpu.VMEM((R, T, LANES), f32),
            pltpu.VMEM((NT, R, T, T), f32),
            pltpu.VMEM((C, R, T, T), bf16),
            pltpu.VMEM((NT, A, R, T, T), bf16),
            pltpu.VMEM((NT, A, R, T, T), bf16),
            dma(()),
            dma((C * NH * pieces,)),
            dma((C * NH * pieces,)),
            dma((C * NH * pieces,)),
            dma((R * pieces,)),
            dma((R * pieces,)),
            dma((C * NH,)),
            dma((NT * A * NH,)),
            dma((C * NH * R,)),
            dma((NT * A * R * NH,)),
        ],
        compiler_params=pltpu.CompilerParams(
            collective_id=0, has_side_effects=True, vmem_limit_bytes=50 * 1024 * 1024
        ),
        cost_estimate=pl.CostEstimate(
            flops=2 * C * T * R * T * kdim, bytes_accessed=8 * 1024 * 1024, transcendentals=0
        ),
    )(
        integrals.reshape(cap * blk, width),
        weights,
    )
    return result.reshape(NT * T, R, T)


def solution(mesh):
    sizes = tuple(mesh.shape[name] for name in ("row", "col", "aux"))
    placed = (
        P("aux", ("row", "col"), None, None),
        P("aux", ("row", "col"), None),
        P("aux", ("row", "col"), None),
        P(),
    )
    return jax.shard_map(
        functools.partial(local, sizes),
        mesh=mesh,
        in_specs=placed,
        out_specs=P(("row", "aux"), None, "col"),
        check_vma=False,
    )
```

```python
import functools

import jax
import jax.numpy as jnp
from jax import lax
from jax.experimental import pallas as pl
from jax.experimental.pallas import tpu as pltpu
from jax.sharding import PartitionSpec as P

MESH = pl.DeviceIdType.MESH
LANES = 128


def weigh(dims, mask_ref, slot_ref, orb_ref, weights):
    MB, OCC, BLK, CAP = dims
    mask, slot = mask_ref[...], slot_ref[...]
    lane_count = mask.shape[1]
    row_ids = lax.broadcasted_iota(jnp.int32, mask.shape, 0)
    lam_ids = lax.broadcasted_iota(jnp.int32, mask.shape, 1)
    code = row_ids * lane_count + lam_ids
    low = lax.broadcasted_iota(jnp.int32, (OCC, LANES), 1) < BLK

    def slot_block(s, half):
        select = jnp.where((mask == 1) & (slot == s), 1, 0)
        position = jnp.sum(select * (code + 1))
        present = jnp.minimum(position, 1)
        place = jnp.maximum(position - 1, 0)
        lam, row = place % lane_count, place // lane_count
        start = pl.multiple_of((lam // 2) * LANES, LANES)
        values = orb_ref[:, pl.ds(start, LANES)].astype(jnp.float32)
        odd = lam % 2
        values = jnp.where(odd == half, values, pltpu.roll(values, BLK, 1))
        return values, row, present

    for p in range(CAP // 2):
        lo, lo_row, lo_here = slot_block(2 * p, 0)
        hi, hi_row, hi_here = slot_block(2 * p + 1, 1)
        for b in range(MB):
            lo_w = jnp.where(lo_row == b, lo_here, 0).astype(jnp.float32)
            hi_w = jnp.where(hi_row == b, hi_here, 0).astype(jnp.float32)
            weights[b * OCC : (b + 1) * OCC, p * LANES : (p + 1) * LANES] = jnp.where(
                low, lo * lo_w, hi * hi_w
            ).astype(jnp.bfloat16)


def row_parts(T):
    return [(0, T // 2), (T // 2, T // 4), (3 * T // 4, T // 4)]


def kernel(
    dims,
    packed_ref,
    weights,
    out_ref,
    panel,
    column,
    block,
    kept,
    send,
    recv_sum,
    recv_turn,
    z_recv,
    z_up,
    z_down,
    row_recv,
    row_send,
    sum_send,
    sum_recv,
    turn_send,
    turn_recv,
):
    R, C, A, MB, OCC, BLK, CAP, KDIM, PIECES = dims
    T = MB * BLK
    parts = row_parts(T)
    NH = len(parts)
    NT = C // A
    half_c = C // 2
    step = KDIM // PIECES
    r, c, a = lax.axis_index("row"), lax.axis_index("col"), lax.axis_index("aux")
    devices = R * C * A
    me = (r * C + c) * A + a

    barrier = pltpu.get_barrier_semaphore()

    def greet(k, _):
        @pl.when(k != me)
        def _():
            pl.semaphore_signal(
                barrier,
                inc=1,
                device_id={"row": k // (C * A), "col": (k // A) % C, "aux": k % A},
                device_id_type=MESH,
            )

        return 0

    lax.fori_loop(0, devices, greet, 0)

    low = lax.broadcasted_iota(jnp.int32, (OCC, LANES), 1) < BLK

    def transform(g, _):
        at = pl.multiple_of(g * 256, 256)
        h = jnp.dot(
            weights[...], packed_ref[:, pl.ds(at, 256)], preferred_element_type=jnp.float32
        )
        for hh in range(T // LANES):
            quarters = []
            for j in range(2):
                b0 = h[2 * hh * OCC : (2 * hh + 1) * OCC, j * LANES : (j + 1) * LANES]
                b1 = h[(2 * hh + 1) * OCC : (2 * hh + 2) * OCC, j * LANES : (j + 1) * LANES]
                quarters.append(jnp.where(low, b0, pltpu.roll(b1, BLK, 1)))
                quarters.append(jnp.where(low, pltpu.roll(b0, BLK, 1), b1))
            tile = jnp.concatenate(quarters, axis=0)
            column[r, hh * LANES : (hh + 1) * LANES, pl.ds(at, 256)] = tile.T.astype(jnp.bfloat16)
        return 0

    def z_copy(src, hh, p, up, own=False):
        start, size = parts[hh]
        lanes = pl.ds(pl.multiple_of(p * step, step), step)
        ref = panel.at[src, pl.ds(start, size), lanes]
        target = jnp.minimum(c + 1, C - 1) if up else jnp.maximum(c - 1, 0)
        index = (src * NH + hh) * PIECES + p
        return pltpu.make_async_remote_copy(
            src_ref=column.at[r, pl.ds(start, size), lanes] if own else ref,
            dst_ref=ref,
            send_sem=(z_up if up else z_down).at[index],
            recv_sem=z_recv.at[index],
            device_id={"row": r, "col": target, "aux": a},
            device_id_type=MESH,
        )

    def row_copy(tile, target, send_index, p):
        ref = column.at[tile, :, pl.ds(pl.multiple_of(p * step, step), step)]
        return pltpu.make_async_remote_copy(
            src_ref=ref,
            dst_ref=ref,
            send_sem=row_send.at[send_index * PIECES + p],
            recv_sem=row_recv.at[tile * PIECES + p],
            device_id={"row": target, "col": c, "aux": a},
            device_id_type=MESH,
        )

    def each_piece(act):
        lax.fori_loop(0, PIECES, lambda p, _: (act(p), 0)[1], 0)

    sends_up = (c < half_c) & (c + 1 < C)
    sends_down = c - 1 >= half_c
    sibling = r + 1 - 2 * (r % 2)
    pairs = R // 2
    peers = [(r + 2 * j) % R for j in range(pairs)]
    far = [(sibling + 2 * j) % R for j in range(pairs)]

    def send_own(hh, p):
        @pl.when(sends_up)
        def _():
            z_copy(c, hh, p, True, True).start()

        @pl.when(sends_down)
        def _():
            z_copy(c, hh, p, False, True).start()

    edge = half_c - 1
    first = step // 256
    lax.fori_loop(0, first, transform, 0)
    pl.semaphore_wait(barrier, devices - 1)

    def make_piece(p, _):
        @pl.when(p > 0)
        def _():
            lax.fori_loop(p * first, (p + 1) * first, transform, 0)

        for j in range(1, pairs):
            row_copy(r, peers[j], j, p).start()
        send_own(0, p)

        @pl.when(c == edge)
        def _():
            for hh in range(1, NH):
                send_own(hh, p)

        row_copy(r, sibling, 0, p).start()
        return 0

    lax.fori_loop(0, PIECES, make_piece, 0)

    @pl.when(c != edge)
    def _():
        for hh in range(1, NH):
            each_piece(lambda p: send_own(hh, p))

    def has_up(src):
        return (src >= 0) & (src < half_c)

    def has_down(src):
        return (src < C) & (c >= half_c)

    def take(src, hh, p, up):
        z_copy(src, hh, p, up).wait_recv()

        @pl.when((c + 1 < C) if up else (c - 1 >= half_c))
        def _():
            z_copy(src, hh, p, up).start()

    passes_down = c - 1 >= half_c

    @pl.when(has_up(c - 1) & (c - 1 == edge))
    def _():
        def every_part(p):
            for hh in range(NH):
                take(c - 1, hh, p, True)

        each_piece(every_part)

    @pl.when(has_up(c - 1) & (c - 1 != edge))
    def _():
        for hh in range(NH):
            each_piece(lambda p: take(c - 1, hh, p, True))

    @pl.when(has_down(c + 1) & passes_down)
    def _():
        for hh in range(NH):
            each_piece(lambda p: take(c + 1, hh, p, False))

    def pass_row(j, p):
        row_copy(peers[j], sibling, j, p).wait_recv()
        row_copy(peers[j], sibling, pairs + j, p).start()

    for j in range(1, pairs):
        each_piece(lambda p: pass_row(j, p))
    for j in range(pairs):
        each_piece(lambda p: row_copy(far[j], sibling, 0, p).wait_recv())

    def sum_copy(src, hh):
        rows = pl.ds(*parts[hh])
        return pltpu.make_async_remote_copy(
            src_ref=send.at[src, :, rows],
            dst_ref=recv_sum.at[src % NT, a, :, rows],
            send_sem=sum_send.at[src * NH + hh],
            recv_sem=sum_recv.at[((src % NT) * A + a) * NH + hh],
            device_id={"row": r, "col": c, "aux": src // NT},
            device_id_type=MESH,
        )

    def turn_copy(src, hh, r2):
        rows = pl.ds(*parts[hh])
        return pltpu.make_async_remote_copy(
            src_ref=send.at[src, r2, rows],
            dst_ref=recv_turn.at[c % NT, a, r, rows],
            send_sem=turn_send.at[(src * NH + hh) * R + r2],
            recv_sem=turn_recv.at[(((c % NT) * A + a) * R + r) * NH + hh],
            device_id={"row": r2, "col": src, "aux": c // NT},
            device_id_type=MESH,
        )

    def settle(src, hh, r2, value, turned):
        rows = pl.ds(*parts[hh])
        send[src, r2, rows] = value.astype(jnp.bfloat16)
        if turned:
            turn_copy(src, hh, r2).start()

        @pl.when(src // NT == a)
        def _():
            kept[src % NT, r2, rows] = value

    def pass_sum(src, hh):
        @pl.when(src // NT != a)
        def _():
            sum_copy(src, hh).start()

    def across(left, right):
        return lax.dot_general(
            left, right, (((1,), (1,)), ((), ())), preferred_element_type=jnp.float32
        )

    def whole(src, turned):
        def one(r2, _):
            value = across(panel[src] if turned else column[r], column[r2])
            for hh, (start, size) in enumerate(parts):
                settle(src, hh, r2, value[start : start + size], turned)
            return 0

        lax.fori_loop(0, R, one, 0)
        for hh in range(NH):
            pass_sum(src, hh)

    def streamed(src, hh, up, taken):
        start, size = parts[hh]

        def piece(p, _):
            @pl.when(p >= taken)
            def _():
                take(src, hh, p, up)

            lanes = pl.ds(pl.multiple_of(p * step, step), step)
            for r2 in range(R):
                value = across(column[r2, :, lanes], panel[src, pl.ds(start, size), lanes])
                old = block[r2, :, :size]
                block[r2, :, :size] = jnp.where(p == 0, value, old + value)
            return 0

        lax.fori_loop(0, PIECES, piece, 0)

        def one(r2, _):
            settle(src, hh, r2, block[r2].T[:size], True)
            return 0

        lax.fori_loop(0, R, one, 0)
        pass_sum(src, hh)

    def ahead(p):
        if C > 2:

            @pl.when(has_up(c - 2))
            def _():
                take(c - 2, 0, p, True)

    block[...] = jnp.zeros_like(block)
    ahead(0)
    whole(c, False)
    ahead(1)

    @pl.when(has_up(c - 1))
    def _():
        whole(c - 1, True)

    ahead(2)

    def nearest_down():
        @pl.when(has_down(c + 1))
        def _():
            @pl.when(jnp.logical_not(passes_down))
            def _():
                for hh in range(NH):
                    each_piece(lambda p: z_copy(c + 1, hh, p, False).wait_recv())

            whole(c + 1, True)

    for d in range(2, C):
        for hh in range(NH):

            @pl.when(has_up(c - d))
            def _():
                streamed(c - d, hh, True, 3 if d == 2 and hh == 0 else 0)

            if d == 2 and hh == 0:
                nearest_down()

            @pl.when(has_down(c + d))
            def _():
                streamed(c + d, hh, False, 0)

    if C == 2:
        nearest_down()

    for t in range(NT):
        tile = a * NT + t
        here = (tile == c) | ((tile < c) & (tile < half_c)) | ((tile > c) & (c >= half_c))

        @pl.when(here)
        def _():
            for hh in range(NH):
                rows = pl.ds(*parts[hh])

                def arrived(other, _):
                    source = (a + other) % A
                    index = (t * A + source) * NH + hh
                    pltpu.make_async_remote_copy(
                        src_ref=recv_sum.at[t, source, :, rows],
                        dst_ref=recv_sum.at[t, source, :, rows],
                        send_sem=sum_send.at[0],
                        recv_sem=sum_recv.at[index],
                        device_id={"row": r, "col": c, "aux": source},
                        device_id_type=MESH,
                    ).wait_recv()
                    kept[t, :, rows] = kept[t, :, rows] + recv_sum[t, source, :, rows].astype(
                        jnp.float32
                    )
                    return 0

                lax.fori_loop(1, A, arrived, 0)
            for r2 in range(R):
                out_ref[t * T : (t + 1) * T, r2 * T : (r2 + 1) * T] = kept[t, r2]

        @pl.when(jnp.logical_not(here))
        def _():
            for r2 in range(R):

                def add(source, total):
                    for hh in range(NH):
                        rows = pl.ds(*parts[hh])
                        index = ((t * A + source) * R + r2) * NH + hh
                        pltpu.make_async_remote_copy(
                            src_ref=recv_turn.at[t, source, r2, rows],
                            dst_ref=recv_turn.at[t, source, r2, rows],
                            send_sem=turn_send.at[0],
                            recv_sem=turn_recv.at[index],
                            device_id={"row": r2, "col": tile, "aux": source},
                            device_id_type=MESH,
                        ).wait_recv()
                    return total + recv_turn[t, source, r2].astype(jnp.float32)

                total = lax.fori_loop(0, A, add, jnp.zeros((T, T), jnp.float32))
                out_ref[t * T : (t + 1) * T, r2 * T : (r2 + 1) * T] = total.T

    def row_sent(p):
        for j in range(1, pairs):
            row_copy(r, peers[j], j, p).wait_send()
            row_copy(peers[j], sibling, pairs + j, p).wait_send()
        row_copy(r, sibling, 0, p).wait_send()

    each_piece(row_sent)
    for hh in range(NH):

        @pl.when(sends_up)
        def _():
            each_piece(lambda p: z_copy(c, hh, p, True, True).wait_send())

        @pl.when(sends_down)
        def _():
            each_piece(lambda p: z_copy(c, hh, p, False, True).wait_send())

    def finish(src, hh, up, turned):
        if turned:

            @pl.when((c + 1 < C) if up else (c - 1 >= half_c))
            def _():
                each_piece(lambda p: z_copy(src, hh, p, up).wait_send())

            lax.fori_loop(0, R, lambda r2, _: (turn_copy(src, hh, r2).wait_send(), 0)[1], 0)

        @pl.when(src // NT != a)
        def _():
            sum_copy(src, hh).wait_send()

    for hh in range(NH):
        finish(c, hh, True, False)
    for d in range(1, C):
        for hh in range(NH):

            @pl.when(has_up(c - d))
            def _():
                finish(c - d, hh, True, True)

            @pl.when(has_down(c + d))
            def _():
                finish(c + d, hh, False, True)


def local(sizes, integrals, block_mask, block_slots, orbitals):
    R, C, A = sizes
    _, cap, blk, width = integrals.shape
    mb = block_mask.shape[1]
    occ = orbitals.shape[0]
    T = mb * blk
    kdim = occ * (width // blk)
    NH, NT, pieces = len(row_parts(T)), C // A, 6
    dims = (R, C, A, mb, occ, blk, cap, kdim, pieces)
    dma = pltpu.SemaphoreType.DMA
    bf16, f32 = jnp.bfloat16, jnp.float32
    vmem = pl.BlockSpec(memory_space=pltpu.VMEM)
    weights = pl.pallas_call(
        functools.partial(weigh, (mb, occ, blk, cap)),
        out_shape=jax.ShapeDtypeStruct((mb * occ, cap * blk), bf16),
        in_specs=[vmem] * 3,
        out_specs=vmem,
    )(
        block_mask.reshape(block_mask.shape[1:]),
        block_slots.reshape(block_slots.shape[1:]),
        orbitals,
    )
    result = pl.pallas_call(
        functools.partial(kernel, dims),
        out_shape=jax.ShapeDtypeStruct((NT * T, R * T), f32),
        in_specs=[vmem] * 2,
        out_specs=vmem,
        scratch_shapes=[
            pltpu.VMEM((C, T, kdim), bf16),
            pltpu.VMEM((R, T, kdim), bf16),
            pltpu.VMEM((R, T, LANES), f32),
            pltpu.VMEM((NT, R, T, T), f32),
            pltpu.VMEM((C, R, T, T), bf16),
            pltpu.VMEM((NT, A, R, T, T), bf16),
            pltpu.VMEM((NT, A, R, T, T), bf16),
            dma((C * NH * pieces,)),
            dma((C * NH * pieces,)),
            dma((C * NH * pieces,)),
            dma((R * pieces,)),
            dma((R * pieces,)),
            dma((C * NH,)),
            dma((NT * A * NH,)),
            dma((C * NH * R,)),
            dma((NT * A * R * NH,)),
        ],
        compiler_params=pltpu.CompilerParams(
            collective_id=0, has_side_effects=True, vmem_limit_bytes=50 * 1024 * 1024
        ),
        cost_estimate=pl.CostEstimate(
            flops=2 * C * T * R * T * kdim, bytes_accessed=8 * 1024 * 1024, transcendentals=0
        ),
    )(
        integrals.reshape(cap * blk, width),
        weights,
    )
    return result.reshape(NT * T, R, T)


def solution(mesh):
    sizes = tuple(mesh.shape[name] for name in ("row", "col", "aux"))
    placed = (
        P("aux", ("row", "col"), None, None),
        P("aux", ("row", "col"), None),
        P("aux", ("row", "col"), None),
        P(),
    )
    return jax.shard_map(
        functools.partial(local, sizes),
        mesh=mesh,
        in_specs=placed,
        out_specs=P(("row", "aux"), None, "col"),
        check_vma=False,
    )
```

```python
import functools

import jax
import jax.numpy as jnp
from jax import lax
from jax.experimental import pallas as pl
from jax.experimental.pallas import tpu as pltpu
from jax.sharding import PartitionSpec as P

MESH = pl.DeviceIdType.MESH
LANES = 128


def weigh(dims, mask_ref, slot_ref, orb_ref, weights):
    MB, OCC, BLK, CAP = dims
    mask, slot = mask_ref[...], slot_ref[...]
    lane_count = mask.shape[1]
    row_ids = lax.broadcasted_iota(jnp.int32, mask.shape, 0)
    lam_ids = lax.broadcasted_iota(jnp.int32, mask.shape, 1)
    code = row_ids * lane_count + lam_ids
    low = lax.broadcasted_iota(jnp.int32, (OCC, LANES), 1) < BLK

    def slot_block(s, half):
        select = jnp.where((mask == 1) & (slot == s), 1, 0)
        position = jnp.sum(select * (code + 1))
        present = jnp.minimum(position, 1)
        place = jnp.maximum(position - 1, 0)
        lam, row = place % lane_count, place // lane_count
        start = pl.multiple_of((lam // 2) * LANES, LANES)
        values = orb_ref[:, pl.ds(start, LANES)].astype(jnp.float32)
        odd = lam % 2
        values = jnp.where(odd == half, values, pltpu.roll(values, BLK, 1))
        return values, row, present

    for p in range(CAP // 2):
        lo, lo_row, lo_here = slot_block(2 * p, 0)
        hi, hi_row, hi_here = slot_block(2 * p + 1, 1)
        for b in range(MB):
            lo_w = jnp.where(lo_row == b, lo_here, 0).astype(jnp.float32)
            hi_w = jnp.where(hi_row == b, hi_here, 0).astype(jnp.float32)
            weights[b * OCC : (b + 1) * OCC, p * LANES : (p + 1) * LANES] = jnp.where(
                low, lo * lo_w, hi * hi_w
            ).astype(jnp.bfloat16)


def row_parts(T):
    return [(0, T // 2), (T // 2, T // 4), (3 * T // 4, T // 4)]


def kernel(
    dims,
    packed_ref,
    weights,
    out_ref,
    panel,
    column,
    block,
    kept,
    send,
    recv_sum,
    recv_turn,
    z_recv,
    z_up,
    z_down,
    row_recv,
    row_send,
    sum_send,
    sum_recv,
    turn_send,
    turn_recv,
):
    R, C, A, MB, OCC, BLK, CAP, KDIM, PIECES = dims
    T = MB * BLK
    parts = row_parts(T)
    NH = len(parts)
    NT = C // A
    half_c = C // 2
    step = KDIM // PIECES
    r, c, a = lax.axis_index("row"), lax.axis_index("col"), lax.axis_index("aux")
    devices = R * C * A
    me = (r * C + c) * A + a

    barrier = pltpu.get_barrier_semaphore()

    def greet(k, _):
        @pl.when(k != me)
        def _():
            pl.semaphore_signal(
                barrier,
                inc=1,
                device_id={"row": k // (C * A), "col": (k // A) % C, "aux": k % A},
                device_id_type=MESH,
            )

        return 0

    lax.fori_loop(0, devices, greet, 0)

    low = lax.broadcasted_iota(jnp.int32, (OCC, LANES), 1) < BLK

    def transform(g, _):
        at = pl.multiple_of(g * 256, 256)
        h = jnp.dot(
            weights[...], packed_ref[:, pl.ds(at, 256)], preferred_element_type=jnp.float32
        )
        for hh in range(T // LANES):
            quarters = []
            for j in range(2):
                b0 = h[2 * hh * OCC : (2 * hh + 1) * OCC, j * LANES : (j + 1) * LANES]
                b1 = h[(2 * hh + 1) * OCC : (2 * hh + 2) * OCC, j * LANES : (j + 1) * LANES]
                quarters.append(jnp.where(low, b0, pltpu.roll(b1, BLK, 1)))
                quarters.append(jnp.where(low, pltpu.roll(b0, BLK, 1), b1))
            tile = jnp.concatenate(quarters, axis=0)
            column[r, hh * LANES : (hh + 1) * LANES, pl.ds(at, 256)] = tile.T.astype(jnp.bfloat16)
        return 0

    def z_copy(src, hh, p, up, own=False):
        start, size = parts[hh]
        lanes = pl.ds(pl.multiple_of(p * step, step), step)
        ref = panel.at[src, pl.ds(start, size), lanes]
        target = jnp.minimum(c + 1, C - 1) if up else jnp.maximum(c - 1, 0)
        index = (src * NH + hh) * PIECES + p
        return pltpu.make_async_remote_copy(
            src_ref=column.at[r, pl.ds(start, size), lanes] if own else ref,
            dst_ref=ref,
            send_sem=(z_up if up else z_down).at[index],
            recv_sem=z_recv.at[index],
            device_id={"row": r, "col": target, "aux": a},
            device_id_type=MESH,
        )

    def row_copy(tile, target, send_index, p):
        ref = column.at[tile, :, pl.ds(pl.multiple_of(p * step, step), step)]
        return pltpu.make_async_remote_copy(
            src_ref=ref,
            dst_ref=ref,
            send_sem=row_send.at[send_index * PIECES + p],
            recv_sem=row_recv.at[tile * PIECES + p],
            device_id={"row": target, "col": c, "aux": a},
            device_id_type=MESH,
        )

    def each_piece(act):
        lax.fori_loop(0, PIECES, lambda p, _: (act(p), 0)[1], 0)

    sends_up = (c < half_c) & (c + 1 < C)
    sends_down = c - 1 >= half_c
    sibling = r + 1 - 2 * (r % 2)
    pairs = R // 2
    peers = [(r + 2 * j) % R for j in range(pairs)]
    far = [(sibling + 2 * j) % R for j in range(pairs)]

    def send_own(hh, p):
        @pl.when(sends_up)
        def _():
            z_copy(c, hh, p, True, True).start()

        @pl.when(sends_down)
        def _():
            z_copy(c, hh, p, False, True).start()

    edge = half_c - 1
    first = step // 256
    lax.fori_loop(0, first, transform, 0)
    pl.semaphore_wait(barrier, devices - 1)

    def make_piece(p, _):
        @pl.when(p > 0)
        def _():
            lax.fori_loop(p * first, (p + 1) * first, transform, 0)

        for j in range(1, pairs):
            row_copy(r, peers[j], j, p).start()
        send_own(0, p)

        @pl.when(c == edge)
        def _():
            for hh in range(1, NH):
                send_own(hh, p)

        row_copy(r, sibling, 0, p).start()
        return 0

    lax.fori_loop(0, PIECES, make_piece, 0)

    @pl.when(c != edge)
    def _():
        for hh in range(1, NH):
            each_piece(lambda p: send_own(hh, p))

    def has_up(src):
        return (src >= 0) & (src < half_c)

    def has_down(src):
        return (src < C) & (c >= half_c)

    def take(src, hh, p, up):
        z_copy(src, hh, p, up).wait_recv()

        @pl.when((c + 1 < C) if up else (c - 1 >= half_c))
        def _():
            z_copy(src, hh, p, up).start()

    passes_down = c - 1 >= half_c

    def pass_row(p):
        for j in range(1, pairs):
            row_copy(peers[j], sibling, j, p).wait_recv()
            row_copy(peers[j], sibling, pairs + j, p).start()

    beside = has_up(c - 1) & (c - 1 == edge)

    @pl.when(beside)
    def _():
        def every_part(p):
            for hh in range(NH):
                take(c - 1, hh, p, True)
            pass_row(p)

        each_piece(every_part)

    @pl.when(has_up(c - 1) & (c - 1 != edge))
    def _():
        for hh in range(NH):
            each_piece(lambda p: take(c - 1, hh, p, True))

    @pl.when(has_down(c + 1) & passes_down)
    def _():
        for hh in range(NH):
            each_piece(lambda p: take(c + 1, hh, p, False))

    @pl.when(jnp.logical_not(beside))
    def _():
        each_piece(pass_row)

    for j in range(pairs):
        each_piece(lambda p: row_copy(far[j], sibling, 0, p).wait_recv())

    def sum_copy(src, hh):
        rows = pl.ds(*parts[hh])
        return pltpu.make_async_remote_copy(
            src_ref=send.at[src, :, rows],
            dst_ref=recv_sum.at[src % NT, a, :, rows],
            send_sem=sum_send.at[src * NH + hh],
            recv_sem=sum_recv.at[((src % NT) * A + a) * NH + hh],
            device_id={"row": r, "col": c, "aux": src // NT},
            device_id_type=MESH,
        )

    def turn_copy(src, hh, r2):
        rows = pl.ds(*parts[hh])
        return pltpu.make_async_remote_copy(
            src_ref=send.at[src, r2, rows],
            dst_ref=recv_turn.at[c % NT, a, r, rows],
            send_sem=turn_send.at[(src * NH + hh) * R + r2],
            recv_sem=turn_recv.at[(((c % NT) * A + a) * R + r) * NH + hh],
            device_id={"row": r2, "col": src, "aux": c // NT},
            device_id_type=MESH,
        )

    def settle(src, hh, r2, value, turned):
        rows = pl.ds(*parts[hh])
        send[src, r2, rows] = value.astype(jnp.bfloat16)
        if turned:
            turn_copy(src, hh, r2).start()

        @pl.when(src // NT == a)
        def _():
            kept[src % NT, r2, rows] = value

    def pass_sum(src, hh):
        @pl.when(src // NT != a)
        def _():
            sum_copy(src, hh).start()

    def across(left, right):
        return lax.dot_general(
            left, right, (((1,), (1,)), ((), ())), preferred_element_type=jnp.float32
        )

    def whole(src, turned):
        def one(r2, _):
            value = across(panel[src] if turned else column[r], column[r2])
            for hh, (start, size) in enumerate(parts):
                settle(src, hh, r2, value[start : start + size], turned)
            return 0

        lax.fori_loop(0, R, one, 0)
        for hh in range(NH):
            pass_sum(src, hh)

    def streamed(src, hh, up, taken):
        start, size = parts[hh]

        def piece(p, _):
            @pl.when(p >= taken)
            def _():
                take(src, hh, p, up)

            lanes = pl.ds(pl.multiple_of(p * step, step), step)
            for r2 in range(R):
                value = across(column[r2, :, lanes], panel[src, pl.ds(start, size), lanes])
                old = block[r2, :, :size]
                block[r2, :, :size] = jnp.where(p == 0, value, old + value)
            return 0

        lax.fori_loop(0, PIECES, piece, 0)

        def one(r2, _):
            settle(src, hh, r2, block[r2].T[:size], True)
            return 0

        lax.fori_loop(0, R, one, 0)
        pass_sum(src, hh)

    def ahead(p):
        if C > 2:

            @pl.when(has_up(c - 2))
            def _():
                take(c - 2, 0, p, True)

    block[...] = jnp.zeros_like(block)
    ahead(0)
    if C == 2:
        whole(c, False)

    @pl.when(has_up(c - 1))
    def _():
        whole(c - 1, True)

    ahead(1)
    ahead(2)

    def nearest_down():
        @pl.when(has_down(c + 1))
        def _():
            @pl.when(jnp.logical_not(passes_down))
            def _():
                for hh in range(NH):
                    each_piece(lambda p: z_copy(c + 1, hh, p, False).wait_recv())

            whole(c + 1, True)

    for d in range(2, C):
        for hh in range(NH):

            @pl.when(has_up(c - d))
            def _():
                streamed(c - d, hh, True, 3 if d == 2 and hh == 0 else 0)

            if d == 2 and hh == 0:
                nearest_down()
                whole(c, False)

            @pl.when(has_down(c + d))
            def _():
                streamed(c + d, hh, False, 0)

    if C == 2:
        nearest_down()

    for t in range(NT):
        tile = a * NT + t
        here = (tile == c) | ((tile < c) & (tile < half_c)) | ((tile > c) & (c >= half_c))

        @pl.when(here)
        def _():
            for hh in range(NH):
                rows = pl.ds(*parts[hh])

                def arrived(other, _):
                    source = (a + other) % A
                    index = (t * A + source) * NH + hh
                    pltpu.make_async_remote_copy(
                        src_ref=recv_sum.at[t, source, :, rows],
                        dst_ref=recv_sum.at[t, source, :, rows],
                        send_sem=sum_send.at[0],
                        recv_sem=sum_recv.at[index],
                        device_id={"row": r, "col": c, "aux": source},
                        device_id_type=MESH,
                    ).wait_recv()
                    kept[t, :, rows] = kept[t, :, rows] + recv_sum[t, source, :, rows].astype(
                        jnp.float32
                    )
                    return 0

                lax.fori_loop(1, A, arrived, 0)
            for r2 in range(R):
                out_ref[t * T : (t + 1) * T, r2 * T : (r2 + 1) * T] = kept[t, r2]

        @pl.when(jnp.logical_not(here))
        def _():
            for r2 in range(R):

                def add(source, total):
                    for hh in range(NH):
                        rows = pl.ds(*parts[hh])
                        index = ((t * A + source) * R + r2) * NH + hh
                        pltpu.make_async_remote_copy(
                            src_ref=recv_turn.at[t, source, r2, rows],
                            dst_ref=recv_turn.at[t, source, r2, rows],
                            send_sem=turn_send.at[0],
                            recv_sem=turn_recv.at[index],
                            device_id={"row": r2, "col": tile, "aux": source},
                            device_id_type=MESH,
                        ).wait_recv()
                    return total + recv_turn[t, source, r2].astype(jnp.float32)

                total = lax.fori_loop(0, A, add, jnp.zeros((T, T), jnp.float32))
                out_ref[t * T : (t + 1) * T, r2 * T : (r2 + 1) * T] = total.T

    def row_sent(p):
        for j in range(1, pairs):
            row_copy(r, peers[j], j, p).wait_send()
            row_copy(peers[j], sibling, pairs + j, p).wait_send()
        row_copy(r, sibling, 0, p).wait_send()

    each_piece(row_sent)
    for hh in range(NH):

        @pl.when(sends_up)
        def _():
            each_piece(lambda p: z_copy(c, hh, p, True, True).wait_send())

        @pl.when(sends_down)
        def _():
            each_piece(lambda p: z_copy(c, hh, p, False, True).wait_send())

    def finish(src, hh, up, turned):
        if turned:

            @pl.when((c + 1 < C) if up else (c - 1 >= half_c))
            def _():
                each_piece(lambda p: z_copy(src, hh, p, up).wait_send())

            lax.fori_loop(0, R, lambda r2, _: (turn_copy(src, hh, r2).wait_send(), 0)[1], 0)

        @pl.when(src // NT != a)
        def _():
            sum_copy(src, hh).wait_send()

    for hh in range(NH):
        finish(c, hh, True, False)
    for d in range(1, C):
        for hh in range(NH):

            @pl.when(has_up(c - d))
            def _():
                finish(c - d, hh, True, True)

            @pl.when(has_down(c + d))
            def _():
                finish(c + d, hh, False, True)


def local(sizes, integrals, block_mask, block_slots, orbitals):
    R, C, A = sizes
    _, cap, blk, width = integrals.shape
    mb = block_mask.shape[1]
    occ = orbitals.shape[0]
    T = mb * blk
    kdim = occ * (width // blk)
    NH, NT, pieces = len(row_parts(T)), C // A, 6
    dims = (R, C, A, mb, occ, blk, cap, kdim, pieces)
    dma = pltpu.SemaphoreType.DMA
    bf16, f32 = jnp.bfloat16, jnp.float32
    vmem = pl.BlockSpec(memory_space=pltpu.VMEM)
    weights = pl.pallas_call(
        functools.partial(weigh, (mb, occ, blk, cap)),
        out_shape=jax.ShapeDtypeStruct((mb * occ, cap * blk), bf16),
        in_specs=[vmem] * 3,
        out_specs=vmem,
    )(
        block_mask.reshape(block_mask.shape[1:]),
        block_slots.reshape(block_slots.shape[1:]),
        orbitals,
    )
    result = pl.pallas_call(
        functools.partial(kernel, dims),
        out_shape=jax.ShapeDtypeStruct((NT * T, R * T), f32),
        in_specs=[vmem] * 2,
        out_specs=vmem,
        scratch_shapes=[
            pltpu.VMEM((C, T, kdim), bf16),
            pltpu.VMEM((R, T, kdim), bf16),
            pltpu.VMEM((R, T, LANES), f32),
            pltpu.VMEM((NT, R, T, T), f32),
            pltpu.VMEM((C, R, T, T), bf16),
            pltpu.VMEM((NT, A, R, T, T), bf16),
            pltpu.VMEM((NT, A, R, T, T), bf16),
            dma((C * NH * pieces,)),
            dma((C * NH * pieces,)),
            dma((C * NH * pieces,)),
            dma((R * pieces,)),
            dma((R * pieces,)),
            dma((C * NH,)),
            dma((NT * A * NH,)),
            dma((C * NH * R,)),
            dma((NT * A * R * NH,)),
        ],
        compiler_params=pltpu.CompilerParams(
            collective_id=0, has_side_effects=True, vmem_limit_bytes=50 * 1024 * 1024
        ),
        cost_estimate=pl.CostEstimate(
            flops=2 * C * T * R * T * kdim, bytes_accessed=8 * 1024 * 1024, transcendentals=0
        ),
    )(
        integrals.reshape(cap * blk, width),
        weights,
    )
    return result.reshape(NT * T, R, T)


def solution(mesh):
    sizes = tuple(mesh.shape[name] for name in ("row", "col", "aux"))
    placed = (
        P("aux", ("row", "col"), None, None),
        P("aux", ("row", "col"), None),
        P("aux", ("row", "col"), None),
        P(),
    )
    return jax.shard_map(
        functools.partial(local, sizes),
        mesh=mesh,
        in_specs=placed,
        out_specs=P(("row", "aux"), None, "col"),
        check_vma=False,
    )
```
